256 devices in a mesh: half: 2 (over y_lo), ctx: 32 (over z, y_hi, core), mp: 4 (over x).
Axes of the slice: x: 4, y: 4 (y_hi: 2, y_lo: 2; y = y_hi * 2 + y_lo), z: 8, core: 2. Of those that a mesh axis runs over, the one named last changes fastest.
Arguments:
- queries: bfloat16 [4096, 5120], P('ctx', ('half', 'mp')), may hold values from -24 to 24
- keys: bfloat16 [4096, 5120], P('ctx', ('half', 'mp')), may hold values from -24 to 24
- values: bfloat16 [4096, 5120], P('ctx', ('half', 'mp')), may hold values from -15 to 15
- token_frames: int32 [4096], P('ctx'), may hold values from 0 to 23, never falling along the last dimension, each value on 1 to 341 neighbouring positions
- frame_actions: int32 [24], replicated, may hold values from 0 to 63
- teacher_resid: bfloat16 [4096, 5120], P('ctx', ('half', 'mp')), may hold values from -2.390625 to 2.390625
- out_weight: bfloat16 [5120, 5120], P(('half', 'mp')), may hold values from -4 to 4
- action_table: bfloat16 [64, 5120], P(None, ('half', 'mp')), may hold values from -2.390625 to 2.390625
- projection: bfloat16 [5120, 2048], P(('half', 'mp')), may hold values from -0.078125 to 0.078125
- student_input: bfloat16 [4096, 2048], P('ctx'), may hold values from -6 to 6
- w_in: bfloat16 [2048, 8192], P('ctx', ('half', 'mp')), may hold values from -0.125 to 0.125
- w_out: bfloat16 [8192, 2048], P(('half', 'mp'), 'ctx'), may hold values from -0.0625 to 0.0625
Outputs:
- grad_in: float32 [2048, 8192], P('ctx', ('half', 'mp'))
- grad_out: float32 [8192, 2048], P(('half', 'mp'), 'ctx')
The draws below stay inside these ranges and needn't reach their ends.
All inputs are finite; a program needn't handle non-finite values.
Results may differ from the reference program's by a relative error of at most 0.024.
Values may be sent and summed in bfloat16 or wider, within the bound.
No kernel may reach another device: no remote copies, remote signals or barrier semaphores. Data moves between devices by JAX's collectives and lax.ppermute only.
A program may use at most 128 MiB of HBM per device.

```python
import math
import jax
import jax.numpy as jnp
import numpy as np
from jax import lax

DT = 5120
HT = 40
DH = 128
DS = 2048
FS = 8192
TOK_DEV = 128
FRAMES = 24
ACTIONS = 64
TOKENS = 4096
N_HALF = 2
N_CTX = 32
N_MP = 4


def draw_queries(key, part):
    key = jax.random.fold_in(key, 1)
    fresh = jax.random.normal(key, (TOKENS, DT), jnp.float32)
    return jnp.clip(fresh, -6.0, 6.0).astype(jnp.bfloat16)


def draw_keys(key, part):
    key = jax.random.fold_in(key, 2)
    noise = jax.random.normal(key, (TOKENS, DT), jnp.float32)
    return jnp.clip(noise, -6.0, 6.0).astype(jnp.bfloat16)


def column_scales(low, high):
    position = jnp.arange(DT, dtype=jnp.float32) / float(DT - 1)
    return jnp.exp(math.log(low) + (math.log(high) - math.log(low)) * position)[None, :]


def draw_out_weight(key, part):
    key = jax.random.fold_in(key, 3)
    fresh = jnp.clip(jax.random.normal(key, (DT, DT), jnp.float32), -4.0, 4.0)
    scales = column_scales(0.35, 3.5)
    return (fresh * scales * (1.0 / math.sqrt(DH))).astype(jnp.bfloat16)


def place_ends(result, stream_key, least, top_value):
    longest = result.shape.index(max(result.shape))
    spots = []
    for shift in (0, 1):
        where = [jax.random.randint(jax.random.fold_in(stream_key, axis), (), 0, length) for axis, length in enumerate(result.shape)]
        where[longest] = (where[longest] + shift) % result.shape[longest]
        spots.append(tuple(where))
    return result.at[spots[0]].set(least).at[spots[1]].set(top_value)


def level_of(key, shape, shards, low, high):
    gain, own = 1.0, jax.random.fold_in(key, 6)
    for dim, blocks in shards:
        steps = jnp.exp(jax.random.uniform(jax.random.fold_in(own, dim), (blocks,), jnp.float32, low / len(shards), high / len(shards)))
        gain = gain * jnp.repeat(steps, shape[dim] // blocks).reshape([-1 if axis == dim else 1 for axis in range(len(shape))])
    return gain


def split_up(number_of, total, most, lean):
    weights = [(1 << 20) // math.isqrt(rank ** lean) + 1 for rank in range(2, number_of + 1)]
    surplus, counts = total - most - (number_of - 1), [1] * (number_of - 1)
    while surplus > 0:
        free = [i for i in range(number_of - 1) if counts[i] < most]
        mass, remaining = sum([weights[i] for i in free]), surplus
        for i in free:
            more = min(most - counts[i], max(1, remaining * weights[i] // mass), surplus)
            counts[i] = counts[i] + more
            surplus = surplus - more
    return np.array([most] + counts)


def ragged(key, amount, total, bound, skew):
    if amount == 2:
        one = jax.random.randint(key, (), max(1, total - bound), min(bound, total - 1) + 1)
        return jnp.stack([one, total - one])
    sizes = jnp.asarray(split_up(amount, total, bound, skew), jnp.int32)
    twos = (amount - 1) // 2
    donor, sink = sizes[1:1 + 2 * twos:2], sizes[2:2 + 2 * twos:2]
    margin = jnp.minimum(donor - 1, bound - sink)
    shifted = jax.random.randint(jax.random.fold_in(key, 1), (twos,), 0, 1 << 20) % (margin + 1)
    sizes = sizes.at[1:1 + 2 * twos:2].set(donor - shifted).at[2:2 + 2 * twos:2].set(sink + shifted)
    return sizes[jax.random.permutation(jax.random.fold_in(key, 2), amount)]


def centred(rng, extent, scale, limit, pieces=(), kind=jnp.bfloat16):
    values = scale * jax.random.normal(rng, extent, jnp.float32)
    if pieces:
        values = values * level_of(rng, extent, pieces, -0.22, 0.18)
    return jnp.clip(values, -limit, limit).astype(kind)


def setup_inputs(seed: int = 0) -> dict:
    streams_of = jax.random.split(jax.random.key(seed), 13)
    queries = draw_queries(jax.random.fold_in(streams_of[12], 71), 0)
    keys = draw_keys(jax.random.fold_in(streams_of[12], 71), 0)
    values = centred(streams_of[2], (TOKENS, DT), 2.5, 15.0, ((0, 32), (1, 8)))
    token_frames = jnp.searchsorted(jnp.cumsum(ragged(streams_of[3], FRAMES, TOKENS, 2 * TOKENS // FRAMES, 1)), jnp.arange(TOKENS), side="right").astype(jnp.int32)
    frame_actions = place_ends(jax.random.randint(streams_of[4], (FRAMES,), 0, ACTIONS), jax.random.fold_in(streams_of[4], 1), 0, ACTIONS - 1).astype(jnp.int32)
    teacher_resid = centred(streams_of[5], (TOKENS, DT), 0.3, 2.390625, ((0, 32), (1, 8)))
    out_weight = draw_out_weight(jax.random.fold_in(streams_of[12], 71), 0)
    action_table = centred(streams_of[7], (ACTIONS, DT), 0.4, 2.390625, ((1, 8),))
    projection = centred(streams_of[8], (DT, DS), DT ** -0.5, 0.078125, ((0, 8),))
    student_input = centred(streams_of[9], (TOKENS, DS), 1.0, 6.0, ((0, 32),))
    w_in = centred(streams_of[10], (DS, FS), DS ** -0.5, 0.125, ((0, 32), (1, 8)))
    w_out = centred(streams_of[11], (FS, DS), FS ** -0.5, 0.0625, ((0, 8), (1, 32)))
    return {"queries": queries, "keys": keys, "values": values, "token_frames": token_frames, "frame_actions": frame_actions, "teacher_resid": teacher_resid, "out_weight": out_weight, "action_table": action_table, "projection": projection, "student_input": student_input, "w_in": w_in, "w_out": w_out}


def gelu_tanh(value):
    return jax.nn.gelu(value, approximate=True)

def reference(queries, keys, values, token_frames, frame_actions, teacher_resid, out_weight, action_table, projection, student_input, w_in, w_out):
    scale = 1.0 / math.sqrt(DH)
    allowed = token_frames[None, :] <= token_frames[:, None]

    def one_head(stacked):
        q_head, k_head, v_head = stacked
        scores = jnp.dot(q_head, k_head.T, preferred_element_type=jnp.float32) * scale
        scores = jnp.where(allowed, scores, -1e+30)
        row_max = lax.optimization_barrier(jnp.max(scores, axis=1, keepdims=True))
        weights = jnp.where(allowed, jnp.exp(scores - row_max), 0.0)
        totals = lax.optimization_barrier(jnp.sum(weights, axis=1, keepdims=True))
        mixed = jnp.dot(weights.astype(jnp.bfloat16), v_head, preferred_element_type=jnp.float32)
        return (mixed / totals).astype(jnp.bfloat16)

    def split_heads(array):
        return array.reshape(TOKENS, HT, DH).transpose(1, 0, 2)
    heads = lax.map(one_head, (split_heads(queries), split_heads(keys), split_heads(values)))
    attended = heads.transpose(1, 0, 2).reshape(TOKENS, DT)
    share_width = DT // (N_HALF * N_MP)

    def share_term(carry, index):
        start = (index * share_width).astype(jnp.int32)
        cols = lax.dynamic_slice_in_dim(attended, start, share_width, 1)
        rows = lax.dynamic_slice_in_dim(out_weight, start, share_width, 0)
        term = jnp.dot(cols, rows, preferred_element_type=jnp.float32)
        term = lax.optimization_barrier(term.astype(jnp.bfloat16)).astype(jnp.float32)
        return (carry + term, None)
    projected, _ = lax.scan(share_term, jnp.zeros((TOKENS, DT), jnp.float32), jnp.arange(N_HALF * N_MP, dtype=jnp.int32))
    token_action = frame_actions[token_frames]
    embedded = action_table[token_action].astype(jnp.float32)
    feature = teacher_resid.astype(jnp.float32) + projected + embedded
    inverse = lax.rsqrt(lax.optimization_barrier(jnp.mean(feature * feature, axis=1, keepdims=True)) + 1e-06)
    normed = (feature * inverse).astype(jnp.bfloat16)
    target = jnp.dot(normed, projection, preferred_element_type=jnp.float32)
    pre = jnp.dot(student_input, w_in, preferred_element_type=jnp.float32)
    activated, pull = jax.vjp(gelu_tanh, pre)
    hidden = activated.astype(jnp.bfloat16)
    error = student_input.astype(jnp.float32) + jnp.dot(hidden, w_out, preferred_element_type=jnp.float32) - target
    grad_rows = (error * (1.0 / math.sqrt(TOKENS))).astype(jnp.bfloat16)
    back = jnp.dot(grad_rows, w_out.T, preferred_element_type=jnp.float32)
    grad_pre = pull(back)[0].astype(jnp.bfloat16)

    def block_terms(carry, index):
        start = (index * TOK_DEV).astype(jnp.int32)
        x_rows = lax.dynamic_slice_in_dim(student_input, start, TOK_DEV, 0)
        pre_rows = lax.dynamic_slice_in_dim(grad_pre, start, TOK_DEV, 0)
        hid_rows = lax.dynamic_slice_in_dim(hidden, start, TOK_DEV, 0)
        out_rows = lax.dynamic_slice_in_dim(grad_rows, start, TOK_DEV, 0)
        term_in = jnp.dot(x_rows.T, pre_rows, preferred_element_type=jnp.float32)
        term_out = jnp.dot(hid_rows.T, out_rows, preferred_element_type=jnp.float32)
        term_in = lax.optimization_barrier(term_in.astype(jnp.bfloat16)).astype(jnp.float32)
        term_out = lax.optimization_barrier(term_out.astype(jnp.bfloat16)).astype(jnp.float32)
        return ((carry[0] + term_in, carry[1] + term_out), None)
    start_sums = (jnp.zeros((DS, FS), jnp.float32), jnp.zeros((FS, DS), jnp.float32))
    sums, _ = lax.scan(block_terms, start_sums, jnp.arange(N_CTX, dtype=jnp.int32))
    return (sums[0], sums[1])
```

```python
import functools
import math

import jax
import jax.numpy as jnp
from jax import lax
from jax.experimental import pallas as pl
from jax.experimental.pallas import tpu as pltpu
from jax.sharding import Mesh, PartitionSpec as P

DH = 128
HEADS = 5
TOK = 128
KV_ROWS = 2 * HEADS * DH
BF = jnp.bfloat16
F32 = jnp.float32
LOG2E = 1.4426950408889634
VMEM_LIMIT = 48 * 1024 * 1024


def call(kernel, outs, scratch=(), smem=0, flops=0, size=0):
    def run(*args):
        specs = [
            pl.BlockSpec(memory_space=pltpu.SMEM if i < smem else pltpu.VMEM)
            for i in range(len(args))
        ]
        return pl.pallas_call(
            kernel,
            out_shape=[jax.ShapeDtypeStruct(s, d) for s, d in outs],
            in_specs=specs,
            out_specs=[pl.BlockSpec(memory_space=pltpu.VMEM) for _ in outs],
            scratch_shapes=list(scratch),
            compiler_params=pltpu.CompilerParams(vmem_limit_bytes=VMEM_LIMIT),
            cost_estimate=pl.CostEstimate(flops=flops, bytes_accessed=size, transcendentals=0),
        )(*args)

    return run


def z_shift(value, step):
    return lax.ppermute(value, "z", [(i, (i + step) % 8) for i in range(8)])


def quad_swap(value, flip):
    return lax.ppermute(value, ("yh", "core"), [(i, i ^ flip) for i in range(4)])


def share_shift(value, flip, step):
    pairs = [
        (h * 4 + m, (h ^ flip) * 4 + (m + step) % 4) for h in range(2) for m in range(4)
    ]
    return lax.ppermute(value, ("half", "mp"), pairs)


SHARE_MOVES = [(0, 0), (1, 2), (0, 2), (1, 1), (1, 3), (0, 1), (0, 3), (1, 0)]


def split3(value):
    high = value.astype(BF).astype(F32)
    rest = value - high
    mid = rest.astype(BF).astype(F32)
    return high, mid, rest - mid


def attend_kernel(*refs):
    q_refs = refs[:4]
    kv_refs = refs[4:11]
    far_k, far_v = refs[11:13]
    out_refs = refs[13:17]
    stat = refs[17]
    scale = LOG2E / math.sqrt(DH)
    stat[...] = jnp.zeros_like(stat)
    frame_rows = [r[KV_ROWS : KV_ROWS + 16, :].astype(F32)[0:1] for r in kv_refs]
    frame_rows.append(far_v[HEADS * DH : HEADS * DH + 16, :].astype(F32)[0:1])
    key_frames = jnp.concatenate(frame_rows, axis=1)
    lane = lax.broadcasted_iota(jnp.int32, (TOK, DH), 1)

    def head_step(head, carry):
        begin = pl.multiple_of(head * DH, DH)
        at_k = pl.ds(begin, DH)
        at_v = pl.ds(pl.multiple_of(begin + HEADS * DH, DH), DH)
        key = jnp.concatenate([r[at_k, :] for r in kv_refs] + [far_k[at_k, :]], axis=0)
        val = jnp.concatenate([r[at_v, :] for r in kv_refs] + [far_v[at_k, :]], axis=0)
        for j in range(4):
            query = q_refs[j][at_k, :]
            row = q_refs[j][HEADS * DH : HEADS * DH + 16, :].astype(F32)[0:1]
            query_frames = jnp.transpose(jnp.broadcast_to(row, (DH, TOK)))[:, 0:1]
            scores = lax.dot_general(
                query, key, (((1,), (1,)), ((), ())), preferred_element_type=F32
            )
            scores = jnp.where(key_frames <= query_frames, scores, -1e30)
            top = jnp.maximum(jnp.max(scores, axis=1, keepdims=True), -1e29)
            weights = jnp.exp2((scores - top) * scale)
            total = jnp.sum(weights, axis=1, keepdims=True)
            mixed = lax.dot_general(
                weights.astype(BF), val, (((1,), (0,)), ((), ())), preferred_element_type=F32
            )
            seen = total > 0.0
            safe = jnp.where(seen, total, 1.0)
            out_refs[j][:, at_k] = (mixed / safe).astype(BF)
            level = jnp.where(seen, top * scale + jnp.log2(safe), -1e30)
            high, mid, low = split3(level)
            stat[j] += (
                jnp.where(lane == head, high, 0.0)
                + jnp.where(lane == head + 16, mid, 0.0)
                + jnp.where(lane == head + 32, low, 0.0)
            )
        return carry

    lax.fori_loop(0, HEADS, head_step, 0)
    for j in range(4):
        out_refs[j][:, HEADS * DH :] = stat[j].astype(BF)


def project_kernel(*refs):
    place = refs[0]
    parts = refs[1:5]
    weight = refs[5]
    outs = refs[6:14]
    stats = [p[:, HEADS * DH :].astype(F32) for p in parts]
    columns = []
    for head in range(HEADS):
        levels = [
            s[:, head : head + 1] + s[:, head + 16 : head + 17] + s[:, head + 32 : head + 33]
            for s in stats
        ]
        top = functools.reduce(jnp.maximum, levels)
        factors = [jnp.exp2(level - top) for level in levels]
        total = sum(factors[1:], factors[0])
        at = slice(head * DH, (head + 1) * DH)
        mixed = sum(f * p[:, at].astype(F32) for f, p in zip(factors, parts))
        columns.append((mixed / total).astype(BF))
    attended = jnp.concatenate(columns, axis=1)
    width = outs[0].shape[1]
    for k, out in enumerate(outs):
        begin = pl.multiple_of(place[k] * width, 128)
        out[...] = jnp.dot(
            attended, weight[:, pl.ds(begin, width)], preferred_element_type=F32
        ).astype(BF)


def feature_kernel(*refs):
    place = refs[0]
    parts = refs[1:9]
    base = refs[9]
    proj = refs[10]
    outs = refs[11:19]
    feature = base[...]
    for part in parts:
        feature = feature + part[...].astype(F32)
    square = jnp.sum(feature * feature, axis=1, keepdims=True)
    turned = jnp.transpose(jnp.broadcast_to(square, (TOK, TOK)))
    high, mid, low = split3(turned[0:16])
    index = lax.broadcasted_iota(jnp.int32, (16, TOK), 0)
    rows = jnp.where(index == 0, high, jnp.where(index == 1, mid, low))
    rows = jnp.concatenate([rows, rows], axis=1).astype(BF)
    narrow = feature.astype(BF)
    for k, out in enumerate(outs):
        begin = pl.multiple_of(place[k] * 256, 256)
        out[0:TOK, :] = jnp.dot(
            narrow, proj[:, pl.ds(begin, 256)], preferred_element_type=F32
        ).astype(BF)
        out[TOK : TOK + 16, :] = rows


def error_kernel(*refs):
    parts = refs[:8]
    student = refs[8]
    out = refs[9]
    target = parts[0][0:TOK, :].astype(F32)
    rows = parts[0][TOK : TOK + 16, :].astype(F32)
    for part in parts[1:]:
        target = target + part[0:TOK, :].astype(F32)
        rows = rows + part[TOK : TOK + 16, :].astype(F32)
    square = rows[0:1, 0:TOK] + rows[1:2, 0:TOK] + rows[2:3, 0:TOK]
    column = jnp.transpose(jnp.broadcast_to(square, (TOK, TOK)))[:, 0:1]
    inverse = lax.rsqrt(column * (1.0 / 5120.0) + 1e-6)
    out[...] = ((student[...] - target * inverse) * (1.0 / 64.0)).astype(BF)


def grad_kernel(*refs):
    share_place, z_place = refs[0:2]
    mine = refs[2:6]
    theirs = refs[6:10]
    w_out_t, slope, hidden_t, x_t = refs[10:14]
    outs = refs[14:22]
    rows = refs[22]
    for half, blocks in enumerate((mine, theirs)):
        for k, block in enumerate(blocks):
            for flip in range(2):
                begin = pl.multiple_of(share_place[flip * 4 + k] * 256, 256)
                for a in range(2):
                    source = (a * 2 + flip) * TOK
                    at = (a * 2 + half) * TOK
                    rows[at : at + TOK, pl.ds(begin, 256)] = block[source : source + TOK, :]
    back = jnp.dot(rows[...], w_out_t[...], preferred_element_type=F32)
    grad_pre = (back * slope[...]).astype(BF)
    for k, out in enumerate(outs):
        begin = pl.multiple_of(z_place[k] * 256, 256)
        out[0:256, :] = jnp.dot(
            x_t[pl.ds(begin, 256), :], grad_pre, preferred_element_type=F32
        ).astype(BF)
        out[256:512, :] = jnp.dot(
            hidden_t[...], rows[:, pl.ds(begin, 256)], preferred_element_type=F32
        ).astype(BF)


def gelu_parts(value):
    k = math.sqrt(2.0 / math.pi)
    square = value * value
    bend = jnp.tanh(k * (value + 0.044715 * value * square))
    out = 0.5 * value * (1.0 + bend)
    slope = 0.5 * (1.0 + bend) + 0.5 * value * (1.0 - bend * bend) * k * (
        1.0 + 3.0 * 0.044715 * square
    )
    return out, slope


def quad_order(blocks, high, low):
    b0, b1, b2, b3 = blocks
    s0, s1 = jnp.where(low, b1, b0), jnp.where(low, b0, b1)
    s2, s3 = jnp.where(low, b3, b2), jnp.where(low, b2, b3)
    return (
        jnp.where(high, s2, s0),
        jnp.where(high, s3, s1),
        jnp.where(high, s0, s2),
        jnp.where(high, s1, s3),
    )


def per_device(
    queries,
    keys,
    values,
    token_frames,
    frame_actions,
    teacher_resid,
    out_weight,
    action_table,
    projection,
    student_input,
    w_in,
    w_out,
):
    half, mp = lax.axis_index("half"), lax.axis_index("mp")
    z, yh, core = lax.axis_index("z"), lax.axis_index("yh"), lax.axis_index("core")
    quad = yh * 2 + core
    share = half * 4 + mp

    frame_rows = jnp.broadcast_to(token_frames.astype(BF)[None, :], (16, TOK))

    def head_rows(array):
        return [array[:, h * DH : (h + 1) * DH] for h in range(HEADS)]

    own_kv = jnp.concatenate(head_rows(keys) + head_rows(values) + [frame_rows], axis=0)
    own_q = jnp.concatenate(head_rows(queries) + [frame_rows], axis=0)
    up1, down1 = z_shift(own_kv, 1), z_shift(own_kv, -1)
    q_y = quad_swap(own_q, 2)
    q_c = quad_swap(own_q, 1)
    q_yc = quad_swap(q_y, 1)
    up2, down2 = z_shift(up1, 1), z_shift(down1, -1)
    up3, down3 = z_shift(up2, 1), z_shift(down2, -1)
    far_k = z_shift(up3[: HEADS * DH], 1)
    far_v = z_shift(down3[HEADS * DH :], -1)

    w_rows = jnp.concatenate([w_in, w_out.T], axis=0)

    def quad_columns(array, flip):
        return lax.dynamic_slice_in_dim(array, (quad ^ flip) * 256, 256, 1)

    pieces = [quad_columns(w_rows, 0)] + [
        quad_swap(quad_columns(w_rows, j), j) for j in (1, 2, 3)
    ]
    ordered = quad_order(pieces, yh == 1, core == 1)
    w_block = jnp.concatenate([o[:64] for o in ordered] + [o[64:] for o in ordered], axis=0)
    w_all = lax.all_gather(w_block, "z", axis=0, tiled=False)
    w_in_full = w_all[:, :256].reshape(2048, 256)
    w_out_t = w_all[:, 256:].reshape(2048, 256)
    x_y = quad_swap(student_input, 2)
    x_c = quad_swap(student_input, 1)
    x_yc = quad_swap(x_y, 1)
    x_plane = jnp.concatenate([student_input, x_c, x_y, x_yc], axis=0)
    pre = jnp.dot(x_plane, w_in_full, preferred_element_type=F32)
    activated, slope = gelu_parts(pre)
    hidden = activated.astype(BF)
    spread = lax.dot_general(
        hidden, w_out_t, (((1,), (1,)), ((), ())), preferred_element_type=F32
    )
    spread = spread.reshape(2, 2, TOK, 2048)
    from_core = quad_swap(spread[:, 1].astype(BF), 1)
    pair_sum = (spread[:, 0] + from_core.astype(F32)).astype(BF).reshape(2 * TOK, 2048)
    share_sum = lax.psum_scatter(pair_sum, ("half", "mp"), scatter_dimension=1, tiled=True)
    from_y = quad_swap(share_sum[TOK:], 2)
    own_cols = lax.dynamic_slice_in_dim(student_input, share * 256, 256, 1)
    student = own_cols.astype(F32) + share_sum[:TOK].astype(F32) + from_y.astype(F32)

    frame_match = token_frames[:, None] == jnp.arange(24, dtype=jnp.int32)[None, :]
    token_action = jnp.sum(jnp.where(frame_match, frame_actions[None, :], 0), axis=1)
    action_hot = (token_action[:, None] == jnp.arange(64, dtype=jnp.int32)[None, :]).astype(BF)
    base = teacher_resid.astype(F32) + jnp.dot(
        action_hot, action_table, preferred_element_type=F32
    )

    partial = call(
        attend_kernel,
        [((TOK, 768), BF)] * 4,
        [pltpu.VMEM((4, TOK, TOK), F32)],
        flops=1400000000,
        size=6000000,
    )(own_q, q_c, q_y, q_yc, own_kv, up1, down1, up2, down2, up3, down3, far_k, far_v)
    parts = [partial[0]] + [quad_swap(partial[j], j) for j in (1, 2, 3)]

    share_place = jnp.stack(
        [(half ^ flip) * 4 + (mp + step) % 4 for flip, step in SHARE_MOVES]
    ).astype(jnp.int32)
    chunks = call(
        project_kernel, [((TOK, 640), BF)] * 8, smem=1, flops=840000000, size=9000000
    )(share_place, *parts, out_weight)
    sums = [chunks[0]] + [
        share_shift(c, flip, step) for c, (flip, step) in zip(chunks[1:], SHARE_MOVES[1:])
    ]
    chunks = call(
        feature_kernel, [((TOK + 16, 256), BF)] * 8, smem=1, flops=340000000, size=5000000
    )(share_place, *sums, base, projection)
    sums = [chunks[0]] + [
        share_shift(c, flip, step) for c, (flip, step) in zip(chunks[1:], SHARE_MOVES[1:])
    ]
    (grad_share,) = call(error_kernel, [((TOK, 256), BF)], flops=1000000, size=800000)(
        *sums, student
    )

    def y_move(value, flip_high, flip_low):
        pairs = [
            (h * 2 + y, (h ^ flip_low) * 2 + (y ^ flip_high)) for h in range(2) for y in range(2)
        ]
        return lax.ppermute(value, ("half", "yh"), pairs)

    along_y = jnp.concatenate(
        [grad_share, y_move(grad_share, 0, 1), y_move(grad_share, 1, 0), y_move(grad_share, 1, 1)],
        axis=0,
    )
    mine = [along_y] + [
        lax.ppermute(along_y, "mp", [(i, (i - k) % 4) for i in range(4)]) for k in (1, 2, 3)
    ]
    theirs = [quad_swap(m, 1) for m in mine]
    col_place = jnp.stack(
        [(half ^ flip) * 4 + (mp + k) % 4 for flip in range(2) for k in range(4)]
    ).astype(jnp.int32)
    z_moves = [4, 3, -3, 2, -2, 1, -1, 0]
    z_place = jnp.stack([(z + k) % 8 for k in z_moves]).astype(jnp.int32)
    grads = call(
        grad_kernel,
        [((512, 256), BF)] * 8,
        [pltpu.VMEM((512, 2048), BF)],
        smem=2,
        flops=1700000000,
        size=10000000,
    )(col_place, z_place, *mine, *theirs, w_out_t, slope, hidden.T, x_plane.T)
    local = dict(zip(z_moves, grads))

    def added(one, two):
        return (one.astype(F32) + two.astype(F32)).astype(BF)

    got_up = z_shift(local[4][:256], 1)
    got_down = z_shift(local[4][256:], -1)
    got_up = z_shift(
        jnp.concatenate([added(got_up, local[3][:256]), local[3][256:]], axis=0), 1
    )
    got_down = z_shift(
        jnp.concatenate([local[-3][:256], added(got_down, local[-3][256:])], axis=0), -1
    )
    got_up = z_shift(added(got_up, local[2]), 1)
    got_down = z_shift(added(got_down, local[-2]), -1)
    got_up = z_shift(added(got_up, local[1]), 1)
    got_down = z_shift(added(got_down, local[-1]), -1)
    block = local[0].astype(F32) + got_up.astype(F32) + got_down.astype(F32)
    block = block.astype(BF)
    block = jnp.concatenate(
        [block[:256].reshape(4, 64, 256), block[256:].T.reshape(4, 64, 256)], axis=1
    )

    def quad_rows(flip):
        return lax.dynamic_index_in_dim(block, quad ^ flip, 0, keepdims=False)

    final = [quad_rows(0)] + [quad_swap(quad_rows(j), j) for j in (1, 2, 3)]
    final = jnp.concatenate(quad_order(final, yh == 1, core == 1), axis=1).astype(F32)
    return (final[:64], final[64:].T)


def solution(mesh):
    shape = mesh.devices.shape
    fine = Mesh(
        mesh.devices.reshape(shape[0], 8, 2, 2, shape[2]), ("half", "z", "yh", "core", "mp")
    )
    ctx = ("z", "yh", "core")
    share = ("half", "mp")
    return jax.shard_map(
        per_device,
        mesh=fine,
        in_specs=(
            P(ctx, share),
            P(ctx, share),
            P(ctx, share),
            P(ctx),
            P(),
            P(ctx, share),
            P(share, None),
            P(None, share),
            P(share, None),
            P(ctx, None),
            P(ctx, share),
            P(share, ctx),
        ),
        out_specs=(P(ctx, share), P(share, ctx)),
        check_vma=False,
    )
```

```python
import functools
import math

import jax
import jax.numpy as jnp
from jax import lax
from jax.experimental import pallas as pl
from jax.experimental.pallas import tpu as pltpu
from jax.sharding import Mesh, PartitionSpec as P

DH = 128
HEADS = 5
TOK = 128
BF = jnp.bfloat16
F32 = jnp.float32
LOG2E = 1.4426950408889634
VMEM_LIMIT = 48 * 1024 * 1024


def call(kernel, outs, scratch=(), smem=0, later=0, flops=0, size=0):
    def run(*args):
        count = len(args)
        spaces = [pltpu.SMEM] * smem + [pltpu.VMEM] * (count - smem - later) + [pl.ANY] * later
        specs = [pl.BlockSpec(memory_space=space) for space in spaces]
        return pl.pallas_call(
            kernel,
            out_shape=[jax.ShapeDtypeStruct(s, d) for s, d in outs],
            in_specs=specs,
            out_specs=[pl.BlockSpec(memory_space=pltpu.VMEM) for _ in outs],
            scratch_shapes=list(scratch),
            compiler_params=pltpu.CompilerParams(vmem_limit_bytes=VMEM_LIMIT),
            cost_estimate=pl.CostEstimate(flops=flops, bytes_accessed=size, transcendentals=0),
        )(*args)

    return run


def z_shift(value, step):
    return lax.ppermute(value, "z", [(i, (i + step) % 8) for i in range(8)])


def quad_swap(value, flip):
    return lax.ppermute(value, ("yh", "core"), [(i, i ^ flip) for i in range(4)])


def split3(value):
    high = value.astype(BF).astype(F32)
    rest = value - high
    mid = rest.astype(BF).astype(F32)
    return high, mid, rest - mid


def message_kernel(queries, values, frames, q_out, v_out):
    row = jnp.broadcast_to(frames[...].astype(F32), (16, TOK)).astype(BF)
    for source, out in ((queries, q_out), (values, v_out)):
        out[0:TOK, :] = source[...]
        for head in range(HEADS):
            out[TOK : TOK + 16, head * DH : (head + 1) * DH] = row


def frames_of(ref):
    return ref[TOK : TOK + 16, 0:TOK].astype(F32)[0:1]


def attend_kernel(*refs):
    q_refs = refs[:4]
    k_refs = refs[4:12]
    v_refs = refs[12:20]
    out_refs = refs[20:24]
    stat = refs[24]
    scale = LOG2E / math.sqrt(DH)
    stat[...] = jnp.zeros_like(stat)
    key_frames = jnp.concatenate([frames_of(r) for r in v_refs], axis=1)
    lane = lax.broadcasted_iota(jnp.int32, (TOK, DH), 1)

    def head_step(head, carry):
        at = pl.ds(pl.multiple_of(head * DH, DH), DH)
        key = jnp.concatenate([r[:, at] for r in k_refs], axis=0)
        val = jnp.concatenate([r[0:TOK, at] for r in v_refs], axis=0)
        for j in range(4):
            query = q_refs[j][0:TOK, at]
            turned = jnp.transpose(jnp.broadcast_to(frames_of(q_refs[j]), (DH, TOK)))
            scores = lax.dot_general(
                query, key, (((1,), (1,)), ((), ())), preferred_element_type=F32
            )
            scores = jnp.where(key_frames <= turned[:, 0:1], scores, -1e30)
            top = jnp.maximum(jnp.max(scores, axis=1, keepdims=True), -1e29)
            weights = jnp.exp2((scores - top) * scale)
            total = jnp.sum(weights, axis=1, keepdims=True)
            mixed = lax.dot_general(
                weights.astype(BF), val, (((1,), (0,)), ((), ())), preferred_element_type=F32
            )
            seen = total > 0.0
            safe = jnp.where(seen, total, 1.0)
            out_refs[j][:, at] = (mixed / safe).astype(BF)
            level = jnp.where(seen, top * scale + jnp.log2(safe), -1e30)
            high, mid, low = split3(level)
            stat[j] += (
                jnp.where(lane == head, high, 0.0)
                + jnp.where(lane == head + 16, mid, 0.0)
                + jnp.where(lane == head + 32, low, 0.0)
            )
        return carry

    lax.fori_loop(0, HEADS, head_step, 0)
    for j in range(4):
        out_refs[j][:, HEADS * DH :] = stat[j].astype(BF)


def project_kernel(*refs):
    parts = refs[:4]
    weight, out = refs[4], refs[6]
    stats = [p[:, HEADS * DH :].astype(F32) for p in parts]
    columns = []
    for head in range(HEADS):
        levels = [
            s[:, head : head + 1] + s[:, head + 16 : head + 17] + s[:, head + 32 : head + 33]
            for s in stats
        ]
        top = functools.reduce(jnp.maximum, levels)
        factors = [jnp.exp2(level - top) for level in levels]
        total = sum(factors[1:], factors[0])
        at = slice(head * DH, (head + 1) * DH)
        mixed = sum(f * p[:, at].astype(F32) for f, p in zip(factors, parts))
        columns.append((mixed / total).astype(BF))
    attended = jnp.concatenate(columns, axis=1)
    width = out.shape[2]
    for k in range(8):
        out[k] = jnp.dot(
            attended, weight[:, k * width : (k + 1) * width], preferred_element_type=F32
        ).astype(BF)


def feature_kernel(parts, base, proj, s_own, s_core, s_y, out):
    feature = base[...]
    for k in range(8):
        feature = feature + parts[k].astype(F32)
    square = jnp.sum(feature * feature, axis=1, keepdims=True)
    turned = jnp.transpose(jnp.broadcast_to(square, (TOK, TOK)))
    high, mid, low = split3(turned[0:16])
    index = lax.broadcasted_iota(jnp.int32, (16, TOK), 0)
    rows = jnp.where(index == 0, high, jnp.where(index == 1, mid, low))
    rows = jnp.concatenate([rows, rows], axis=1).astype(BF)
    narrow = feature.astype(BF)
    for k in range(8):
        at = slice(k * 256, (k + 1) * 256)
        out[k, 0:TOK, :] = jnp.dot(narrow, proj[:, at], preferred_element_type=F32).astype(BF)
        out[k, TOK : 2 * TOK, :] = (
            s_own[0:TOK, at].astype(F32) + s_core[0:TOK, at].astype(F32) + s_y[:, at].astype(F32)
        ).astype(BF)
        out[k, 2 * TOK : 2 * TOK + 16, :] = rows


def error_kernel(parts, own_cols, out):
    target, student, rows = 0.0, own_cols[...].astype(F32), 0.0
    for k in range(8):
        target = target + parts[k, 0:TOK, :].astype(F32)
        student = student + parts[k, TOK : 2 * TOK, :].astype(F32)
        rows = rows + parts[k, 2 * TOK : 2 * TOK + 16, :].astype(F32)
    square = rows[0:1, 0:TOK] + rows[1:2, 0:TOK] + rows[2:3, 0:TOK]
    column = jnp.transpose(jnp.broadcast_to(square, (TOK, TOK)))[:, 0:1]
    inverse = lax.rsqrt(column * (1.0 / 5120.0) + 1e-6)
    out[...] = ((student - target * inverse) * (1.0 / 64.0)).astype(BF)


def pieces_kernel(place, w_in, w_out_t, *rest):
    for j, out in enumerate(rest[4:]):
        at = pl.ds(pl.multiple_of(place[j] * 256, 256), 256)
        out[0:64, :] = w_in[:, at]
        out[64:128, :] = w_out_t[:, at]


def merge_kernel(place, p0, p1, p2, p3, *rest):
    out = rest[4]
    for j, piece in enumerate((p0, p1, p2, p3)):
        begin = pl.multiple_of(place[j] * 64, 64)
        out[pl.ds(begin, 64), :] = piece[0:64, :]
        out[pl.ds(begin + 256, 64), :] = piece[64:128, :]


def student_kernel(x0, x1, x2, x3, weight, later, slope, hidden_t, local, to_core):
    pre = jnp.zeros((4 * TOK, 256), F32)
    for z in range(8):
        at = slice(z * 256, (z + 1) * 256)
        rows = jnp.concatenate([x0[:, at], x1[:, at], x2[:, at], x3[:, at]], axis=0)
        pre = pre + jnp.dot(rows, weight[z, 0:256, :], preferred_element_type=F32)
    activated, slope[...] = gelu_parts(pre)
    hidden_t[...] = jnp.transpose(activated).astype(BF)
    hidden = activated.astype(BF)
    for z in range(8):
        at = slice(z * 256, (z + 1) * 256)
        spread = lax.dot_general(
            hidden,
            weight[z, 256:512, :],
            (((1,), (1,)), ((), ())),
            preferred_element_type=F32,
        ).astype(BF)
        for a in range(2):
            local[a * TOK : (a + 1) * TOK, at] = spread[2 * a * TOK : (2 * a + 1) * TOK]
            to_core[a * TOK : (a + 1) * TOK, at] = spread[(2 * a + 1) * TOK : (2 * a + 2) * TOK]


def grad_kernel(*refs):
    share_place, z_place = refs[0:2]
    mine = refs[2:6]
    theirs = refs[6:10]
    weight, slope, hidden_t = refs[10:13]
    x_refs = refs[13:17]
    outs = refs[17:25]
    rows = refs[25]
    for half, blocks in enumerate((mine, theirs)):
        for k, block in enumerate(blocks):
            for flip in range(2):
                begin = pl.multiple_of(share_place[flip * 4 + k] * 256, 256)
                for a in range(2):
                    source = (a * 2 + flip) * TOK
                    at = (a * 2 + half) * TOK
                    rows[at : at + TOK, pl.ds(begin, 256)] = block[source : source + TOK, :]
    back = jnp.zeros((4 * TOK, 256), F32)
    for z in range(8):
        back = back + jnp.dot(
            rows[:, z * 256 : (z + 1) * 256], weight[z, 256:512, :], preferred_element_type=F32
        )
    grad_pre = jnp.transpose(back * slope[...]).astype(BF)
    for k, out in enumerate(outs):
        at = pl.ds(pl.multiple_of(z_place[k] * 256, 256), 256)
        inputs = jnp.concatenate([r[:, at] for r in x_refs], axis=0)
        out[0:256, :] = jnp.dot(grad_pre, inputs, preferred_element_type=F32).astype(BF)
        out[256:512, :] = jnp.dot(
            hidden_t[...], rows[:, at], preferred_element_type=F32
        ).astype(BF)


def turn_kernel(place, local, up, down, o0, o1, o2, o3, block):
    total = local[...].astype(F32) + up[...].astype(F32) + down[...].astype(F32)
    block[...] = jnp.transpose(total)
    for j, out in enumerate((o0, o1, o2, o3)):
        at = pl.ds(pl.multiple_of(place[j] * 64, 64), 64)
        out[...] = block[at, :].astype(BF)


def final_kernel(place, p0, p1, p2, p3, grad_in, grad_out_t):
    for j, part in enumerate((p0, p1, p2, p3)):
        at = pl.ds(pl.multiple_of(place[j] * 256, 256), 256)
        piece = part[...].astype(F32)
        grad_in[:, at] = piece[:, 0:256]
        grad_out_t[:, at] = piece[:, 256:512]


def gelu_parts(value):
    k = math.sqrt(2.0 / math.pi)
    square = value * value
    bend = jnp.tanh(k * (value + 0.044715 * value * square))
    out = 0.5 * value * (1.0 + bend)
    slope = 0.5 * (1.0 + bend) + 0.5 * value * (1.0 - bend * bend) * k * (
        1.0 + 3.0 * 0.044715 * square
    )
    return out, slope


def per_device(
    queries,
    keys,
    values,
    token_frames,
    frame_actions,
    teacher_resid,
    out_weight,
    action_table,
    projection,
    student_input,
    w_in,
    w_out,
):
    half, mp = lax.axis_index("half"), lax.axis_index("mp")
    z, yh, core = lax.axis_index("z"), lax.axis_index("yh"), lax.axis_index("core")
    quad = yh * 2 + core
    share = half * 4 + mp

    col_place = jnp.stack(
        [(half ^ flip) * 4 + ((mp + k) & 3) for flip in range(2) for k in range(4)]
    ).astype(jnp.int32)
    z_moves = [4, 3, -3, 2, -2, 1, -1, 0]
    z_place = jnp.stack([(z + k) & 7 for k in z_moves]).astype(jnp.int32)
    quad_place = jnp.stack([quad ^ j for j in range(4)]).astype(jnp.int32)

    own_q, own_v = call(message_kernel, [((TOK + 16, 640), BF)] * 2, size=660000)(
        queries, values, token_frames.reshape(1, TOK)
    )
    k_up, k_down = z_shift(keys, 1), z_shift(keys, -1)
    v_up, v_down = z_shift(own_v, 1), z_shift(own_v, -1)
    all_k, all_v = [keys, k_up, k_down], [own_v, v_up, v_down]
    q_y = quad_swap(own_q, 2)
    q_c = quad_swap(own_q, 1)
    q_yc = quad_swap(q_y, 1)

    k_up, k_down = z_shift(k_up, 1), z_shift(k_down, -1)
    v_up, v_down = z_shift(v_up, 1), z_shift(v_down, -1)
    all_k += [k_up, k_down]
    all_v += [v_up, v_down]
    pieces = call(pieces_kernel, [((TOK, 256), BF)] * 4, smem=1, later=4, size=500000)(
        quad_place, w_in, w_out.T, *all_k[1:3], *all_v[1:3]
    )
    pieces = [pieces[0]] + [quad_swap(pieces[j], j) for j in (1, 2, 3)]
    (w_block,) = call(merge_kernel, [((512, 256), BF)], smem=1, later=4, size=500000)(
        quad_place, *pieces, k_up, k_down, v_up, v_down
    )
    w_all = lax.all_gather(w_block, "z", axis=0, tiled=False)
    x_own, k_up, k_down = lax.optimization_barrier((student_input, k_up, k_down))
    x_y = quad_swap(x_own, 2)
    x_c = quad_swap(x_own, 1)
    x_yc = quad_swap(x_y, 1)
    x_parts = (student_input, x_c, x_y, x_yc)
    k_up, k_down = z_shift(k_up, 1), z_shift(k_down, -1)
    v_up, v_down = z_shift(v_up, 1), z_shift(v_down, -1)
    all_k += [k_up, k_down]
    all_v += [v_up, v_down]
    all_k.append(z_shift(k_up, 1))
    all_v.append(z_shift(v_down, -1))

    frame_match = token_frames[:, None] == jnp.arange(24, dtype=jnp.int32)[None, :]
    token_action = jnp.sum(jnp.where(frame_match, frame_actions[None, :], 0), axis=1)
    action_hot = (token_action[:, None] == jnp.arange(64, dtype=jnp.int32)[None, :]).astype(BF)
    base = teacher_resid.astype(F32) + jnp.dot(
        action_hot, action_table, preferred_element_type=F32
    )

    partial = call(
        attend_kernel,
        [((TOK, 768), BF)] * 4,
        [pltpu.VMEM((4, TOK, TOK), F32)],
        flops=1400000000,
        size=6000000,
    )(own_q, q_c, q_y, q_yc, *all_k, *all_v)
    parts = [partial[0]] + [quad_swap(partial[j], j) for j in (1, 2, 3)]
    slope, hidden_t, local, to_core = call(
        student_kernel,
        [((512, 256), F32), ((256, 512), BF), ((256, 2048), BF), ((256, 2048), BF)],
        later=1,
    )(*x_parts, w_all, parts[1])
    from_core = quad_swap(to_core, 1)
    to_y = (local[TOK:].astype(F32) + from_core[TOK:].astype(F32)).astype(BF)
    from_y = quad_swap(to_y, 2)
    (chunks,) = call(
        project_kernel, [((8, TOK, 640), BF)], later=1, flops=840000000, size=9000000
    )(*parts, out_weight, from_core)
    sums = lax.all_to_all(chunks, ("half", "mp"), split_axis=0, concat_axis=0, tiled=True)
    (chunks,) = call(
        feature_kernel, [((8, 2 * TOK + 16, 256), BF)], flops=340000000, size=5000000
    )(sums, base, projection, local, from_core, from_y)
    sums = lax.all_to_all(chunks, ("half", "mp"), split_axis=0, concat_axis=0, tiled=True)
    own_cols = lax.dynamic_slice_in_dim(student_input, share * 256, 256, 1)
    (grad_share,) = call(error_kernel, [((TOK, 256), BF)], flops=1000000, size=800000)(
        sums, own_cols
    )

    def y_move(value, flip_high, flip_low):
        pairs = [
            (h * 2 + y, (h ^ flip_low) * 2 + (y ^ flip_high)) for h in range(2) for y in range(2)
        ]
        return lax.ppermute(value, ("half", "yh"), pairs)

    along_y = jnp.concatenate(
        [grad_share, y_move(grad_share, 0, 1), y_move(grad_share, 1, 0), y_move(grad_share, 1, 1)],
        axis=0,
    )
    mine = [along_y] + [
        lax.ppermute(along_y, "mp", [(i, (i - k) % 4) for i in range(4)]) for k in (1, 2, 3)
    ]
    theirs = [quad_swap(m, 1) for m in mine]
    grads = call(
        grad_kernel,
        [((512, 256), BF)] * 8,
        [pltpu.VMEM((512, 2048), BF)],
        smem=2,
        flops=1700000000,
        size=10000000,
    )(col_place, z_place, *mine, *theirs, w_all, slope, hidden_t, *x_parts)
    local = dict(zip(z_moves, grads))

    def added(one, two):
        return (one.astype(F32) + two.astype(F32)).astype(BF)

    up = z_shift(local[4][:256], 1)
    down = z_shift(local[4][256:], -1)
    up = z_shift(jnp.concatenate([added(up, local[3][:256]), local[3][256:]], axis=0), 1)
    down = z_shift(jnp.concatenate([local[-3][:256], added(down, local[-3][256:])], axis=0), -1)
    for k in (2, 1):
        up = z_shift(added(up, local[k]), 1)
        down = z_shift(added(down, local[-k]), -1)
    blocks = call(
        turn_kernel,
        [((64, 512), BF)] * 4,
        [pltpu.VMEM((256, 512), F32)],
        smem=1,
        flops=1000000,
        size=1000000,
    )(quad_place, local[0], up, down)
    blocks = [blocks[0]] + [quad_swap(blocks[j], j) for j in (1, 2, 3)]
    grad_in, grad_out_t = call(
        final_kernel, [((64, 1024), F32)] * 2, smem=1, flops=1000000, size=1000000
    )(quad_place, *blocks)
    return grad_in, grad_out_t.T


def solution(mesh):
    shape = mesh.devices.shape
    fine = Mesh(
        mesh.devices.reshape(shape[0], 8, 2, 2, shape[2]), ("half", "z", "yh", "core", "mp")
    )
    ctx = ("z", "yh", "core")
    share = ("half", "mp")
    return jax.shard_map(
        per_device,
        mesh=fine,
        in_specs=(
            P(ctx, share),
            P(ctx, share),
            P(ctx, share),
            P(ctx),
            P(),
            P(ctx, share),
            P(share, None),
            P(None, share),
            P(share, None),
            P(ctx, None),
            P(ctx, share),
            P(share, ctx),
        ),
        out_specs=(P(ctx, share), P(share, ctx)),
        check_vma=False,
    )
```

```python
import functools
import math

import jax
import jax.numpy as jnp
from jax import lax
from jax.experimental import pallas as pl
from jax.experimental.pallas import tpu as pltpu
from jax.sharding import Mesh, PartitionSpec as P

DH = 128
HEADS = 5
TOK = 128
BF = jnp.bfloat16
F32 = jnp.float32
LOG2E = 1.4426950408889634
VMEM_LIMIT = 24 * 1024 * 1024


def call(kernel, outs, scratch=(), smem=0, later=0, flops=0, size=0):
    def run(*args):
        count = len(args)
        spaces = [pltpu.SMEM] * smem + [pltpu.VMEM] * (count - smem - later) + [pl.ANY] * later
        specs = [pl.BlockSpec(memory_space=space) for space in spaces]
        return pl.pallas_call(
            kernel,
            out_shape=[jax.ShapeDtypeStruct(s, d) for s, d in outs],
            in_specs=specs,
            out_specs=[pl.BlockSpec(memory_space=pltpu.VMEM) for _ in outs],
            scratch_shapes=list(scratch),
            compiler_params=pltpu.CompilerParams(vmem_limit_bytes=VMEM_LIMIT),
            cost_estimate=pl.CostEstimate(flops=flops, bytes_accessed=size, transcendentals=0),
        )(*args)

    return run


def z_shift(value, step):
    return lax.ppermute(value, "z", [(i, (i + step) % 8) for i in range(8)])


def quad_swap(value, flip):
    return lax.ppermute(value, ("yh", "core"), [(i, i ^ flip) for i in range(4)])


def split3(value):
    high = value.astype(BF).astype(F32)
    rest = value - high
    mid = rest.astype(BF).astype(F32)
    return high, mid, rest - mid


def message_kernel(queries, keys, values, frames, q_out, kv_out):
    row = jnp.broadcast_to(frames[...].astype(F32), (16, TOK)).astype(BF)
    q_out[0:TOK, :] = queries[...]
    kv_out[0:TOK, :] = keys[...]
    kv_out[TOK : 2 * TOK, :] = values[...]
    for head in range(HEADS):
        at = slice(head * DH, (head + 1) * DH)
        q_out[TOK : TOK + 16, at] = row
        kv_out[2 * TOK : 2 * TOK + 16, at] = row


def attend_kernel(q0, q1, q2, q3, kv, o0, o1, o2, o3, stat):
    q_refs, out_refs = (q0, q1, q2, q3), (o0, o1, o2, o3)
    scale = LOG2E / math.sqrt(DH)
    stat[...] = jnp.zeros_like(stat)
    key_frames = jnp.concatenate(
        [kv[z, 2 * TOK : 2 * TOK + 16, 0:TOK].astype(F32)[0:1] for z in range(8)], axis=1
    )
    lane = lax.broadcasted_iota(jnp.int32, (TOK, DH), 1)

    def head_step(head, carry):
        at = pl.ds(pl.multiple_of(head * DH, DH), DH)
        key = jnp.concatenate([kv[z, 0:TOK, at] for z in range(8)], axis=0)
        val = jnp.concatenate([kv[z, TOK : 2 * TOK, at] for z in range(8)], axis=0)
        for j in range(4):
            query = q_refs[j][0:TOK, at]
            row = q_refs[j][TOK : TOK + 16, 0:TOK].astype(F32)[0:1]
            turned = jnp.transpose(jnp.broadcast_to(row, (DH, TOK)))
            scores = lax.dot_general(
                query, key, (((1,), (1,)), ((), ())), preferred_element_type=F32
            )
            scores = jnp.where(key_frames <= turned[:, 0:1], scores, -1e30)
            top = jnp.maximum(jnp.max(scores, axis=1, keepdims=True), -1e29)
            weights = jnp.exp2((scores - top) * scale)
            total = jnp.sum(weights, axis=1, keepdims=True)
            mixed = lax.dot_general(
                weights.astype(BF), val, (((1,), (0,)), ((), ())), preferred_element_type=F32
            )
            seen = total > 0.0
            safe = jnp.where(seen, total, 1.0)
            out_refs[j][:, at] = (mixed / safe).astype(BF)
            level = jnp.where(seen, top * scale + jnp.log2(safe), -1e30)
            high, mid, low = split3(level)
            stat[j] += (
                jnp.where(lane == head, high, 0.0)
                + jnp.where(lane == head + 16, mid, 0.0)
                + jnp.where(lane == head + 32, low, 0.0)
            )
        return carry

    lax.fori_loop(0, HEADS, head_step, 0)
    for j in range(4):
        out_refs[j][:, HEADS * DH :] = stat[j].astype(BF)


def project_kernel(*refs):
    parts = refs[:4]
    weight, out = refs[4:6]
    stats = [p[:, HEADS * DH :].astype(F32) for p in parts]
    columns = []
    for head in range(HEADS):
        levels = [
            s[:, head : head + 1] + s[:, head + 16 : head + 17] + s[:, head + 32 : head + 33]
            for s in stats
        ]
        top = functools.reduce(jnp.maximum, levels)
        factors = [jnp.exp2(level - top) for level in levels]
        total = sum(factors[1:], factors[0])
        at = slice(head * DH, (head + 1) * DH)
        mixed = sum(f * p[:, at].astype(F32) for f, p in zip(factors, parts))
        columns.append((mixed / total).astype(BF))
    attended = jnp.concatenate(columns, axis=1)
    width = out.shape[2]
    for k in range(8):
        out[k] = jnp.dot(
            attended, weight[:, k * width : (k + 1) * width], preferred_element_type=F32
        ).astype(BF)


def feature_kernel(parts, base, proj, out):
    feature = base[...]
    for k in range(8):
        feature = feature + parts[k].astype(F32)
    square = jnp.sum(feature * feature, axis=1, keepdims=True)
    turned = jnp.transpose(jnp.broadcast_to(square, (TOK, TOK)))
    high, mid, low = split3(turned[0:16])
    index = lax.broadcasted_iota(jnp.int32, (16, TOK), 0)
    rows = jnp.where(index == 0, high, jnp.where(index == 1, mid, low))
    rows = jnp.concatenate([rows, rows], axis=1).astype(BF)
    narrow = feature.astype(BF)
    for k in range(8):
        at = slice(k * 256, (k + 1) * 256)
        out[k, 0:TOK, :] = jnp.dot(narrow, proj[:, at], preferred_element_type=F32).astype(BF)
        out[k, TOK : TOK + 16, :] = rows


def error_kernel(parts, s_own, s_y, out):
    target, rows = 0.0, 0.0
    for k in range(8):
        target = target + parts[k, 0:TOK, :].astype(F32)
        rows = rows + parts[k, TOK : TOK + 16, :].astype(F32)
    square = rows[0:1, 0:TOK] + rows[1:2, 0:TOK] + rows[2:3, 0:TOK]
    column = jnp.transpose(jnp.broadcast_to(square, (TOK, TOK)))[:, 0:1]
    inverse = lax.rsqrt(column * (1.0 / 5120.0) + 1e-6)
    student = s_own[...] + s_y[...].astype(F32)
    out[...] = ((student - target * inverse) * (1.0 / 64.0)).astype(BF)


def pair_kernel(one, two, out):
    for k in range(8):
        at = slice(k * 256, (k + 1) * 256)
        out[k] = (one[:, at].astype(F32) + two[:, at].astype(F32)).astype(BF)


def student_sum_kernel(parts, own_cols, s_own, to_y):
    here, there = own_cols[...].astype(F32), 0.0
    for k in range(8):
        here = here + parts[k, 0:TOK, :].astype(F32)
        there = there + parts[k, TOK : 2 * TOK, :].astype(F32)
    s_own[...] = here
    to_y[...] = there.astype(BF)


def pieces_kernel(place, w_in, w_out_t, later, *outs):
    for j, out in enumerate(outs):
        at = pl.ds(pl.multiple_of(place[j] * 256, 256), 256)
        out[0:64, :] = w_in[:, at]
        out[64:128, :] = w_out_t[:, at]


def merge_kernel(place, p0, p1, p2, p3, out):
    for j, piece in enumerate((p0, p1, p2, p3)):
        begin = pl.multiple_of(place[j] * 64, 64)
        out[pl.ds(begin, 64), :] = piece[0:64, :]
        out[pl.ds(begin + 256, 64), :] = piece[64:128, :]


def student_kernel(x0, x1, x2, x3, weight, later, slope, hidden_t, local, to_core):
    pre = jnp.zeros((4 * TOK, 256), F32)
    for z in range(8):
        at = slice(z * 256, (z + 1) * 256)
        rows = jnp.concatenate([x0[:, at], x1[:, at], x2[:, at], x3[:, at]], axis=0)
        pre = pre + jnp.dot(rows, weight[z, 0:256, :], preferred_element_type=F32)
    activated, slope[...] = gelu_parts(pre)
    hidden_t[...] = jnp.transpose(activated).astype(BF)
    hidden = activated.astype(BF)
    for z in range(8):
        at = slice(z * 256, (z + 1) * 256)
        spread = lax.dot_general(
            hidden,
            weight[z, 256:512, :],
            (((1,), (1,)), ((), ())),
            preferred_element_type=F32,
        ).astype(BF)
        for a in range(2):
            local[a * TOK : (a + 1) * TOK, at] = spread[2 * a * TOK : (2 * a + 1) * TOK]
            to_core[a * TOK : (a + 1) * TOK, at] = spread[(2 * a + 1) * TOK : (2 * a + 2) * TOK]


def grad_kernel(quad_place, z_place, gathered, weight, slope, hidden_t, x0, x1, x2, x3, *rest):
    x_refs, outs, rows = (x0, x1, x2, x3), rest[:8], rest[8]
    for j in range(4):
        for k in range(8):
            rows[j * TOK : (j + 1) * TOK, k * 256 : (k + 1) * 256] = gathered[
                quad_place[j] * 8 + k
            ]
    back = jnp.zeros((4 * TOK, 256), F32)
    for z in range(8):
        back = back + jnp.dot(
            rows[:, z * 256 : (z + 1) * 256], weight[z, 256:512, :], preferred_element_type=F32
        )
    grad_pre = jnp.transpose(back * slope[...]).astype(BF)
    for k, out in enumerate(outs):
        at = pl.ds(pl.multiple_of(z_place[k] * 256, 256), 256)
        inputs = jnp.concatenate([r[:, at] for r in x_refs], axis=0)
        out[0:256, :] = jnp.dot(grad_pre, inputs, preferred_element_type=F32).astype(BF)
        out[256:512, :] = jnp.dot(
            hidden_t[...], rows[:, at], preferred_element_type=F32
        ).astype(BF)


def turn_kernel(place, local, up, down, o0, o1, o2, o3, block):
    total = local[...].astype(F32) + up[...].astype(F32) + down[...].astype(F32)
    block[...] = jnp.transpose(total)
    for j, out in enumerate((o0, o1, o2, o3)):
        at = pl.ds(pl.multiple_of(place[j] * 64, 64), 64)
        out[...] = block[at, :].astype(BF)


def final_kernel(place, p0, p1, p2, p3, grad_in, grad_out_t):
    for j, part in enumerate((p0, p1, p2, p3)):
        at = pl.ds(pl.multiple_of(place[j] * 256, 256), 256)
        piece = part[...].astype(F32)
        grad_in[:, at] = piece[:, 0:256]
        grad_out_t[:, at] = piece[:, 256:512]


def gelu_parts(value):
    k = math.sqrt(2.0 / math.pi)
    square = value * value
    bend = jnp.tanh(k * (value + 0.044715 * value * square))
    out = 0.5 * value * (1.0 + bend)
    slope = 0.5 * (1.0 + bend) + 0.5 * value * (1.0 - bend * bend) * k * (
        1.0 + 3.0 * 0.044715 * square
    )
    return out, slope


def per_device(
    queries,
    keys,
    values,
    token_frames,
    frame_actions,
    teacher_resid,
    out_weight,
    action_table,
    projection,
    student_input,
    w_in,
    w_out,
):
    half, mp = lax.axis_index("half"), lax.axis_index("mp")
    z, yh, core = lax.axis_index("z"), lax.axis_index("yh"), lax.axis_index("core")
    quad = yh * 2 + core
    share = half * 4 + mp

    z_moves = [4, 3, -3, 2, -2, 1, -1, 0]
    z_place = jnp.stack([(z + k) & 7 for k in z_moves]).astype(jnp.int32)
    quad_place = jnp.stack([quad ^ j for j in range(4)]).astype(jnp.int32)

    own_q, own_kv = call(
        message_kernel, [((TOK + 16, 640), BF), ((2 * TOK + 16, 640), BF)], size=1000000
    )(queries, keys, values, token_frames.reshape(1, TOK))
    kv = lax.all_gather(own_kv, "z", axis=0, tiled=False)

    pieces = call(pieces_kernel, [((TOK, 256), BF)] * 4, smem=1, later=1, size=500000)(
        quad_place, w_in, w_out.T, own_kv
    )
    pieces = [pieces[0]] + [quad_swap(pieces[j], j) for j in (1, 2, 3)]
    (w_block,) = call(merge_kernel, [((512, 256), BF)], smem=1, size=500000)(
        quad_place, *pieces
    )
    w_all = lax.all_gather(w_block, "z", axis=0, tiled=False)
    q_y = quad_swap(own_q, 2)
    q_c = quad_swap(own_q, 1)
    q_yc = quad_swap(q_y, 1)
    x_own, q_y = lax.optimization_barrier((student_input, q_y))
    x_y = quad_swap(x_own, 2)
    x_c = quad_swap(x_own, 1)
    x_yc = quad_swap(x_y, 1)
    x_parts = (student_input, x_c, x_y, x_yc)

    frame_match = token_frames[:, None] == jnp.arange(24, dtype=jnp.int32)[None, :]
    token_action = jnp.sum(jnp.where(frame_match, frame_actions[None, :], 0), axis=1)
    action_hot = (token_action[:, None] == jnp.arange(64, dtype=jnp.int32)[None, :]).astype(BF)
    base = teacher_resid.astype(F32) + jnp.dot(
        action_hot, action_table, preferred_element_type=F32
    )

    partial = call(
        attend_kernel,
        [((TOK, 768), BF)] * 4,
        [pltpu.VMEM((4, TOK, TOK), F32)],
        flops=1400000000,
        size=6000000,
    )(own_q, q_c, q_y, q_yc, kv)
    parts = [partial[0]] + [quad_swap(partial[j], j) for j in (1, 2, 3)]
    (chunks,) = call(project_kernel, [((8, TOK, 640), BF)], flops=840000000, size=9000000)(
        *parts, out_weight
    )
    slope, hidden_t, local, to_core = call(
        student_kernel,
        [((512, 256), F32), ((256, 512), BF), ((256, 2048), BF), ((256, 2048), BF)],
        later=1,
    )(*x_parts, w_all, chunks)
    sums = lax.all_to_all(chunks, ("half", "mp"), split_axis=0, concat_axis=0, tiled=True)
    (s_chunks,) = call(pair_kernel, [((8, 256, 256), BF)], flops=1000000, size=3000000)(
        local, quad_swap(to_core, 1)
    )
    s_sums = lax.all_to_all(s_chunks, ("half", "mp"), split_axis=0, concat_axis=0, tiled=True)
    own_cols = lax.dynamic_slice_in_dim(student_input, share * 256, 256, 1)
    s_own, to_y = call(
        student_sum_kernel, [((TOK, 256), F32), ((TOK, 256), BF)], flops=1000000, size=1500000
    )(s_sums, own_cols)
    (chunks,) = call(
        feature_kernel, [((8, TOK + 16, 256), BF)], flops=340000000, size=5000000
    )(sums, base, projection)
    sums = lax.all_to_all(chunks, ("half", "mp"), split_axis=0, concat_axis=0, tiled=True)
    (grad_share,) = call(error_kernel, [((TOK, 256), BF)], flops=1000000, size=800000)(
        sums, s_own, quad_swap(to_y, 2)
    )

    gathered = lax.all_gather(
        grad_share, ("yh", "core", "half", "mp"), axis=0, tiled=False
    )
    grads = call(
        grad_kernel,
        [((512, 256), BF)] * 8,
        [pltpu.VMEM((512, 2048), BF)],
        smem=2,
        flops=1700000000,
        size=10000000,
    )(quad_place, z_place, gathered, w_all, slope, hidden_t, *x_parts)
    local = dict(zip(z_moves, grads))

    def added(one, two):
        return (one.astype(F32) + two.astype(F32)).astype(BF)

    up = z_shift(local[4][:256], 1)
    down = z_shift(local[4][256:], -1)
    up = z_shift(jnp.concatenate([added(up, local[3][:256]), local[3][256:]], axis=0), 1)
    down = z_shift(jnp.concatenate([local[-3][:256], added(down, local[-3][256:])], axis=0), -1)
    for k in (2, 1):
        up = z_shift(added(up, local[k]), 1)
        down = z_shift(added(down, local[-k]), -1)
    blocks = call(
        turn_kernel,
        [((64, 512), BF)] * 4,
        [pltpu.VMEM((256, 512), F32)],
        smem=1,
        flops=1000000,
        size=1000000,
    )(quad_place, local[0], up, down)
    blocks = [blocks[0]] + [quad_swap(blocks[j], j) for j in (1, 2, 3)]
    grad_in, grad_out_t = call(
        final_kernel, [((64, 1024), F32)] * 2, smem=1, flops=1000000, size=1000000
    )(quad_place, *blocks)
    return grad_in, grad_out_t.T


def solution(mesh):
    shape = mesh.devices.shape
    fine = Mesh(
        mesh.devices.reshape(shape[0], 8, 2, 2, shape[2]), ("half", "z", "yh", "core", "mp")
    )
    ctx = ("z", "yh", "core")
    share = ("half", "mp")
    return jax.shard_map(
        per_device,
        mesh=fine,
        in_specs=(
            P(ctx, share),
            P(ctx, share),
            P(ctx, share),
            P(ctx),
            P(),
            P(ctx, share),
            P(share, None),
            P(None, share),
            P(share, None),
            P(ctx, None),
            P(ctx, share),
            P(share, ctx),
        ),
        out_specs=(P(ctx, share), P(share, ctx)),
        check_vma=False,
    )
```

```python
import functools
import math

import jax
import jax.numpy as jnp
from jax import lax
from jax.experimental import pallas as pl
from jax.experimental.pallas import tpu as pltpu
from jax.sharding import Mesh, PartitionSpec as P

DH = 128
HEADS = 5
TOK = 128
BF = jnp.bfloat16
F32 = jnp.float32
LOG2E = 1.4426950408889634
VMEM_LIMIT = 24 * 1024 * 1024


def call(kernel, outs, scratch=(), smem=0, later=0, flops=0, size=0):
    def run(*args):
        count = len(args)
        spaces = [pltpu.SMEM] * smem + [pltpu.VMEM] * (count - smem - later) + [pl.ANY] * later
        specs = [pl.BlockSpec(memory_space=space) for space in spaces]
        return pl.pallas_call(
            kernel,
            out_shape=[jax.ShapeDtypeStruct(s, d) for s, d in outs],
            in_specs=specs,
            out_specs=[pl.BlockSpec(memory_space=pltpu.VMEM) for _ in outs],
            scratch_shapes=list(scratch),
            compiler_params=pltpu.CompilerParams(vmem_limit_bytes=VMEM_LIMIT),
            cost_estimate=pl.CostEstimate(flops=flops, bytes_accessed=size, transcendentals=0),
        )(*args)

    return run


def z_shift(value, step):
    return lax.ppermute(value, "z", [(i, (i + step) % 8) for i in range(8)])


def quad_swap(value, flip):
    return lax.ppermute(value, ("yh", "core"), [(i, i ^ flip) for i in range(4)])


def share_shift(value, flip, step):
    pairs = [
        (h * 4 + m, (h ^ flip) * 4 + (m + step) % 4) for h in range(2) for m in range(4)
    ]
    return lax.ppermute(value, ("half", "mp"), pairs)


SHARE_MOVES = [(0, 0), (1, 2), (0, 2), (1, 1), (1, 3), (0, 1), (0, 3), (1, 0)]


def split3(value):
    high = value.astype(BF).astype(F32)
    rest = value - high
    mid = rest.astype(BF).astype(F32)
    return high, mid, rest - mid


def message_kernel(queries, keys, values, frames, q_out, kv_out):
    row = jnp.broadcast_to(frames[...].astype(F32), (16, TOK)).astype(BF)
    q_out[0:TOK, :] = queries[...]
    kv_out[0:TOK, :] = keys[...]
    kv_out[TOK : 2 * TOK, :] = values[...]
    for head in range(HEADS):
        at = slice(head * DH, (head + 1) * DH)
        q_out[TOK : TOK + 16, at] = row
        kv_out[2 * TOK : 2 * TOK + 16, at] = row


def attend_kernel(*refs):
    q_refs, kv_refs, far_k, far_v = refs[:4], refs[4:11], refs[11], refs[12]
    keep, send, stat = refs[13:16]
    outs = [keep.at[0], keep.at[1], send.at[0], send.at[1]]
    scale = LOG2E / math.sqrt(DH)
    stat[...] = jnp.zeros_like(stat)
    key_frames = jnp.concatenate(
        [r[2 * TOK : 2 * TOK + 16, 0:TOK].astype(F32)[0:1] for r in kv_refs]
        + [far_v[TOK : TOK + 16, 0:TOK].astype(F32)[0:1]],
        axis=1,
    )
    lane = lax.broadcasted_iota(jnp.int32, (TOK, DH), 1)

    def head_step(head, carry):
        at = pl.ds(pl.multiple_of(head * DH, DH), DH)
        key = jnp.concatenate([r[0:TOK, at] for r in kv_refs] + [far_k[:, at]], axis=0)
        val = jnp.concatenate(
            [r[TOK : 2 * TOK, at] for r in kv_refs] + [far_v[0:TOK, at]], axis=0
        )
        for j in range(4):
            query = q_refs[j][0:TOK, at]
            row = q_refs[j][TOK : TOK + 16, 0:TOK].astype(F32)[0:1]
            turned = jnp.transpose(jnp.broadcast_to(row, (DH, TOK)))
            scores = lax.dot_general(
                query, key, (((1,), (1,)), ((), ())), preferred_element_type=F32
            )
            scores = jnp.where(key_frames <= turned[:, 0:1], scores, -1e30)
            top = jnp.maximum(jnp.max(scores, axis=1, keepdims=True), -1e29)
            weights = jnp.exp2((scores - top) * scale)
            total = jnp.sum(weights, axis=1, keepdims=True)
            mixed = lax.dot_general(
                weights.astype(BF), val, (((1,), (0,)), ((), ())), preferred_element_type=F32
            )
            seen = total > 0.0
            safe = jnp.where(seen, total, 1.0)
            outs[j][:, at] = (mixed / safe).astype(BF)
            level = jnp.where(seen, top * scale + jnp.log2(safe), -1e30)
            high, mid, low = split3(level)
            stat[j] += (
                jnp.where(lane == head, high, 0.0)
                + jnp.where(lane == head + 16, mid, 0.0)
                + jnp.where(lane == head + 32, low, 0.0)
            )
        return carry

    lax.fori_loop(0, HEADS, head_step, 0)
    for j in range(4):
        outs[j][:, HEADS * DH :] = stat[j].astype(BF)


def merged(parts):
    stats = [p[:, HEADS * DH :].astype(F32) for p in parts]
    columns, levels = [], []
    for head in range(HEADS):
        each = [
            s[:, head : head + 1] + s[:, head + 16 : head + 17] + s[:, head + 32 : head + 33]
            for s in stats
        ]
        top = functools.reduce(jnp.maximum, each)
        factors = [jnp.exp2(level - top) for level in each]
        total = sum(factors[1:], factors[0])
        at = slice(head * DH, (head + 1) * DH)
        mixed = sum(f * p[:, at].astype(F32) for f, p in zip(factors, parts))
        columns.append((mixed / total).astype(BF))
        levels.append(top + jnp.log2(total))
    return columns, levels


def merge_pair_kernel(keep, got, mine, other):
    lane = lax.broadcasted_iota(jnp.int32, (TOK, DH), 1)
    for b, out in enumerate((mine, other)):
        columns, levels = merged([keep.at[b], got.at[b]])
        out[:, 0 : HEADS * DH] = jnp.concatenate(columns, axis=1)
        stat = jnp.zeros((TOK, DH), F32)
        for head, level in enumerate(levels):
            high, mid, low = split3(level)
            stat += (
                jnp.where(lane == head, high, 0.0)
                + jnp.where(lane == head + 16, mid, 0.0)
                + jnp.where(lane == head + 32, low, 0.0)
            )
        out[:, HEADS * DH :] = stat.astype(BF)


def project_kernel(place, mine, got, weight, *rest):
    outs, attended = rest[:8], rest[8]
    step = pl.program_id(0)

    @pl.when(step == 0)
    def _():
        attended[...] = jnp.concatenate(merged([mine, got])[0], axis=1)

    product = jnp.dot(attended[...], weight[...], preferred_element_type=F32).astype(BF)
    for k, out in enumerate(outs):

        @pl.when(step == k)
        def _(out=out):
            out[...] = product


def project(place, mine, got, weight):
    part = pl.BlockSpec((TOK, 768), lambda k, p: (0, 0))
    return pl.pallas_call(
        project_kernel,
        grid_spec=pltpu.PrefetchScalarGridSpec(
            num_scalar_prefetch=1,
            grid=(8,),
            in_specs=[part, part, pl.BlockSpec((640, 640), lambda k, p: (0, p[k]))],
            out_specs=[pl.BlockSpec((TOK, 640), lambda k, p: (0, 0)) for _ in range(8)],
            scratch_shapes=[pltpu.VMEM((TOK, 640), BF)],
        ),
        out_shape=[jax.ShapeDtypeStruct((TOK, 640), BF)] * 8,
        compiler_params=pltpu.CompilerParams(vmem_limit_bytes=VMEM_LIMIT),
        cost_estimate=pl.CostEstimate(flops=840000000, bytes_accessed=9000000, transcendentals=0),
    )(place, mine, got, weight)


def feature_kernel(place, *refs):
    parts, base, proj, outs = refs[:8], refs[8], refs[9], refs[10:18]
    feature = base[...]
    for part in parts:
        feature = feature + part[...].astype(F32)
    square = jnp.sum(feature * feature, axis=1, keepdims=True)
    turned = jnp.transpose(jnp.broadcast_to(square, (TOK, TOK)))
    high, mid, low = split3(turned[0:16])
    index = lax.broadcasted_iota(jnp.int32, (16, TOK), 0)
    rows = jnp.where(index == 0, high, jnp.where(index == 1, mid, low))
    rows = jnp.concatenate([rows, rows], axis=1).astype(BF)
    narrow = feature.astype(BF)
    for k, out in enumerate(outs):
        at = pl.ds(pl.multiple_of(place[k] * 256, 256), 256)
        out[0:TOK, :] = jnp.dot(narrow, proj[:, at], preferred_element_type=F32).astype(BF)
        out[TOK : TOK + 16, :] = rows


def error_kernel(*refs):
    parts, s_own, s_y, out = refs[:8], refs[8], refs[9], refs[10]
    target, rows = 0.0, 0.0
    for part in parts:
        target = target + part[0:TOK, :].astype(F32)
        rows = rows + part[TOK : TOK + 16, :].astype(F32)
    square = rows[0:1, 0:TOK] + rows[1:2, 0:TOK] + rows[2:3, 0:TOK]
    column = jnp.transpose(jnp.broadcast_to(square, (TOK, TOK)))[:, 0:1]
    inverse = lax.rsqrt(column * (1.0 / 5120.0) + 1e-6)
    student = s_own[...] + s_y[...].astype(F32)
    out[...] = ((student - target * inverse) * (1.0 / 64.0)).astype(BF)


def pieces_kernel(place, w_in, w_out_t, *rest):
    for j, out in enumerate(rest[2:]):
        at = pl.ds(pl.multiple_of(place[j] * 256, 256), 256)
        out[0:64, :] = w_in[:, at]
        out[64:128, :] = w_out_t[:, at]


def merge_kernel(place, p0, p1, p2, p3, *rest):
    out = rest[-1]
    for j, piece in enumerate((p0, p1, p2, p3)):
        begin = pl.multiple_of(place[j] * 64, 64)
        out[pl.ds(begin, 64), :] = piece[0:64, :]
        out[pl.ds(begin + 256, 64), :] = piece[64:128, :]


def student_kernel(place, x0, x1, x2, x3, weight, later, slope, hidden_t, spread_out):
    pre = jnp.zeros((4 * TOK, 256), F32)
    for z in range(8):
        at = slice(z * 256, (z + 1) * 256)
        rows = jnp.concatenate([x0[:, at], x1[:, at], x2[:, at], x3[:, at]], axis=0)
        pre = pre + jnp.dot(rows, weight[z, 0:256, :], preferred_element_type=F32)
    activated, slope[...] = gelu_parts(pre)
    hidden_t[...] = jnp.transpose(activated).astype(BF)
    hidden = activated.astype(BF)
    for z in range(8):
        spread = lax.dot_general(
            hidden,
            weight[z, 256:512, :],
            (((1,), (1,)), ((), ())),
            preferred_element_type=F32,
        ).astype(BF)
        for j in range(4):
            begin = (j // 2) * TOK
            spread_out[place[j % 2] * 8 + z, begin : begin + TOK, :] = spread[
                j * TOK : (j + 1) * TOK
            ]


def grad_kernel(*refs):
    share_place, z_place = refs[0:2]
    mine = refs[2:6]
    theirs = refs[6:10]
    weight, slope, hidden_t = refs[10:13]
    x_refs = refs[13:17]
    outs = refs[17:25]
    rows = refs[25]
    for half, blocks in enumerate((mine, theirs)):
        for k, block in enumerate(blocks):
            for flip in range(2):
                begin = pl.multiple_of(share_place[flip * 4 + k] * 256, 256)
                for a in range(2):
                    source = (a * 2 + flip) * TOK
                    at = (a * 2 + half) * TOK
                    rows[at : at + TOK, pl.ds(begin, 256)] = block[source : source + TOK, :]
    back = jnp.zeros((4 * TOK, 256), F32)
    for z in range(8):
        back = back + jnp.dot(
            rows[:, z * 256 : (z + 1) * 256], weight[z, 256:512, :], preferred_element_type=F32
        )
    grad_pre = jnp.transpose(back * slope[...]).astype(BF)
    for k, out in enumerate(outs):
        at = pl.ds(pl.multiple_of(z_place[k] * 256, 256), 256)
        inputs = jnp.concatenate([r[:, at] for r in x_refs], axis=0)
        out[0:256, :] = jnp.dot(grad_pre, inputs, preferred_element_type=F32).astype(BF)
        out[256:512, :] = jnp.dot(
            hidden_t[...], rows[:, at], preferred_element_type=F32
        ).astype(BF)


def turn_kernel(place, local, up, down, o0, o1, o2, o3, block):
    total = local[...].astype(F32) + up[...].astype(F32) + down[...].astype(F32)
    block[...] = jnp.transpose(total)
    for j, out in enumerate((o0, o1, o2, o3)):
        at = pl.ds(pl.multiple_of(place[j] * 64, 64), 64)
        out[...] = block[at, :].astype(BF)


def final_kernel(place, p0, p1, p2, p3, grad_in, grad_out_t):
    for j, part in enumerate((p0, p1, p2, p3)):
        at = pl.ds(pl.multiple_of(place[j] * 256, 256), 256)
        piece = part[...].astype(F32)
        grad_in[:, at] = piece[:, 0:256]
        grad_out_t[:, at] = piece[:, 256:512]


def gelu_parts(value):
    k = math.sqrt(2.0 / math.pi)
    square = value * value
    bend = jnp.tanh(k * (value + 0.044715 * value * square))
    out = 0.5 * value * (1.0 + bend)
    slope = 0.5 * (1.0 + bend) + 0.5 * value * (1.0 - bend * bend) * k * (
        1.0 + 3.0 * 0.044715 * square
    )
    return out, slope


def per_device(
    queries,
    keys,
    values,
    token_frames,
    frame_actions,
    teacher_resid,
    out_weight,
    action_table,
    projection,
    student_input,
    w_in,
    w_out,
):
    half, mp = lax.axis_index("half"), lax.axis_index("mp")
    z, yh, core = lax.axis_index("z"), lax.axis_index("yh"), lax.axis_index("core")
    quad = yh * 2 + core
    share = half * 4 + mp

    share_place = jnp.stack(
        [(half ^ flip) * 4 + ((mp + step) & 3) for flip, step in SHARE_MOVES]
    ).astype(jnp.int32)
    col_place = jnp.stack(
        [(half ^ flip) * 4 + ((mp + k) & 3) for flip in range(2) for k in range(4)]
    ).astype(jnp.int32)
    z_moves = [4, 3, -3, 2, -2, 1, -1, 0]
    z_place = jnp.stack([(z + k) & 7 for k in z_moves]).astype(jnp.int32)
    quad_place = jnp.stack([quad ^ j for j in range(4)]).astype(jnp.int32)

    own_q, own_kv = call(
        message_kernel, [((TOK + 16, 640), BF), ((2 * TOK + 16, 640), BF)], size=1000000
    )(queries, keys, values, token_frames.reshape(1, TOK))
    up1, down1 = z_shift(own_kv, 1), z_shift(own_kv, -1)
    pieces = call(pieces_kernel, [((TOK, 256), BF)] * 4, smem=1, later=2, size=500000)(
        quad_place, w_in, w_out.T, up1, down1
    )
    pieces = [pieces[0]] + [quad_swap(pieces[j], j) for j in (1, 2, 3)]
    q_own, x_own, up1, down1 = lax.optimization_barrier((own_q, student_input, up1, down1))
    q_y = quad_swap(q_own, 2)
    q_c = quad_swap(q_own, 1)
    q_yc = quad_swap(q_y, 1)
    up2, down2 = z_shift(up1, 1), z_shift(down1, -1)
    x_y = quad_swap(x_own, 2)
    x_c = quad_swap(x_own, 1)
    up3, down3 = z_shift(up2, 1), z_shift(down2, -1)
    x_y, x_c, q_c, q_yc, up3, down3 = lax.optimization_barrier(
        (x_y, x_c, q_c, q_yc, up3, down3)
    )
    x_yc = quad_swap(x_y, 1)
    x_parts = (student_input, x_c, x_y, x_yc)
    far_k, far_v = z_shift(up3[:TOK], 1), z_shift(down3[TOK:], -1)
    (w_block,) = call(merge_kernel, [((512, 256), BF)], smem=1, later=2, size=500000)(
        quad_place, *pieces, far_k, far_v
    )
    w_all = lax.all_gather(w_block, "z", axis=0, tiled=False)

    frame_match = token_frames[:, None] == jnp.arange(24, dtype=jnp.int32)[None, :]
    token_action = jnp.sum(jnp.where(frame_match, frame_actions[None, :], 0), axis=1)
    action_hot = (token_action[:, None] == jnp.arange(64, dtype=jnp.int32)[None, :]).astype(BF)
    base = teacher_resid.astype(F32) + jnp.dot(
        action_hot, action_table, preferred_element_type=F32
    )

    keep, away = call(
        attend_kernel,
        [((2, TOK, 768), BF)] * 2,
        [pltpu.VMEM((4, TOK, TOK), F32)],
        flops=1400000000,
        size=6000000,
    )(
        own_q, q_c, q_y, q_yc,
        own_kv, up1, down1, up2, down2, up3, down3, far_k, far_v,
    )
    got = quad_swap(away, 2)
    core_place = jnp.stack([core, core ^ 1]).astype(jnp.int32)
    slope, hidden_t, spread = call(
        student_kernel,
        [((512, 256), F32), ((256, 512), BF), ((16, 256, 256), BF)],
        smem=1,
        later=1,
    )(core_place, *x_parts, w_all, got)
    share_sum = lax.psum_scatter(
        spread, ("core", "half", "mp"), scatter_dimension=0, tiled=True
    ).reshape(256, 256)
    mine, other = call(merge_pair_kernel, [((TOK, 768), BF)] * 2, size=1500000)(keep, got)
    chunks = project(share_place, mine, quad_swap(other, 1), out_weight)
    sums = [chunks[0]] + [
        share_shift(c, flip, step) for c, (flip, step) in zip(chunks[1:], SHARE_MOVES[1:])
    ]
    chunks = call(
        feature_kernel, [((TOK + 16, 256), BF)] * 8, smem=1, flops=340000000, size=5000000
    )(share_place, *sums, base, projection)
    sums = [chunks[0]] + [
        share_shift(c, flip, step) for c, (flip, step) in zip(chunks[1:], SHARE_MOVES[1:])
    ]
    share_sum, sums[3] = lax.optimization_barrier((share_sum, sums[3]))
    own_cols = lax.dynamic_slice_in_dim(student_input, share * 256, 256, 1)
    s_own = own_cols.astype(F32) + share_sum[:TOK].astype(F32)
    s_y = quad_swap(share_sum[TOK:], 2)
    (grad_share,) = call(error_kernel, [((TOK, 256), BF)], flops=1000000, size=800000)(
        *sums, s_own, s_y
    )

    def y_move(value, flip_high, flip_low):
        pairs = [
            (h * 2 + y, (h ^ flip_low) * 2 + (y ^ flip_high)) for h in range(2) for y in range(2)
        ]
        return lax.ppermute(value, ("half", "yh"), pairs)

    along_y = jnp.concatenate(
        [grad_share, y_move(grad_share, 0, 1), y_move(grad_share, 1, 0), y_move(grad_share, 1, 1)],
        axis=0,
    )
    mine = [along_y] + [
        lax.ppermute(along_y, "mp", [(i, (i - k) % 4) for i in range(4)]) for k in (1, 2, 3)
    ]
    theirs = [quad_swap(m, 1) for m in mine]
    grads = call(
        grad_kernel,
        [((512, 256), BF)] * 8,
        [pltpu.VMEM((512, 2048), BF)],
        smem=2,
        flops=1700000000,
        size=10000000,
    )(col_place, z_place, *mine, *theirs, w_all, slope, hidden_t, *x_parts)
    local = dict(zip(z_moves, grads))

    def added(one, two):
        return (one.astype(F32) + two.astype(F32)).astype(BF)

    up = z_shift(local[4][:256], 1)
    down = z_shift(local[4][256:], -1)
    up = z_shift(jnp.concatenate([added(up, local[3][:256]), local[3][256:]], axis=0), 1)
    down = z_shift(jnp.concatenate([local[-3][:256], added(down, local[-3][256:])], axis=0), -1)
    for k in (2, 1):
        up = z_shift(added(up, local[k]), 1)
        down = z_shift(added(down, local[-k]), -1)
    blocks = call(
        turn_kernel,
        [((64, 512), BF)] * 4,
        [pltpu.VMEM((256, 512), F32)],
        smem=1,
        flops=1000000,
        size=1000000,
    )(quad_place, local[0], up, down)
    blocks = [blocks[0]] + [quad_swap(blocks[j], j) for j in (1, 2, 3)]
    grad_in, grad_out_t = call(
        final_kernel, [((64, 1024), F32)] * 2, smem=1, flops=1000000, size=1000000
    )(quad_place, *blocks)
    return grad_in, grad_out_t.T


def solution(mesh):
    shape = mesh.devices.shape
    fine = Mesh(
        mesh.devices.reshape(shape[0], 8, 2, 2, shape[2]), ("half", "z", "yh", "core", "mp")
    )
    ctx = ("z", "yh", "core")
    share = ("half", "mp")
    return jax.shard_map(
        per_device,
        mesh=fine,
        in_specs=(
            P(ctx, share),
            P(ctx, share),
            P(ctx, share),
            P(ctx),
            P(),
            P(ctx, share),
            P(share, None),
            P(None, share),
            P(share, None),
            P(ctx, None),
            P(ctx, share),
            P(share, ctx),
        ),
        out_specs=(P(ctx, share), P(share, ctx)),
        check_vma=False,
    )
```

```python
import functools
import math

import jax
import jax.numpy as jnp
from jax import lax
from jax.experimental import pallas as pl
from jax.experimental.pallas import tpu as pltpu
from jax.sharding import Mesh, PartitionSpec as P

DH = 128
HEADS = 5
TOK = 128
BF = jnp.bfloat16
F32 = jnp.float32
LOG2E = 1.4426950408889634
MIB = 1024 * 1024


def call(kernel, outs, scratch=(), fetch=0, later=0, flops=0, size=0, vmem=44):
    def body(*refs):
        held = refs[:fetch]
        tail = refs[len(refs) - fetch - (1 if fetch else 0) :]
        rest = refs[fetch : len(refs) - len(tail)]
        copies = [
            pltpu.make_async_copy(source, target, tail[-1].at[i])
            for i, (source, target) in enumerate(zip(held, tail))
        ]
        for copy in copies:
            copy.start()
        for copy in copies:
            copy.wait()
        kernel(*tail[:fetch], *rest)

    def run(*args):
        count = len(args) - fetch - later
        spaces = [pltpu.HBM] * fetch + [pltpu.VMEM] * count + [pl.ANY] * later
        buffers = [pltpu.VMEM(a.shape, a.dtype) for a in args[:fetch]]
        if fetch:
            buffers.append(pltpu.SemaphoreType.DMA((fetch,)))
        return pl.pallas_call(
            body,
            out_shape=[jax.ShapeDtypeStruct(s, d) for s, d in outs],
            in_specs=[pl.BlockSpec(memory_space=space) for space in spaces],
            out_specs=[pl.BlockSpec(memory_space=pltpu.VMEM) for _ in outs],
            scratch_shapes=list(scratch) + buffers,
            compiler_params=pltpu.CompilerParams(vmem_limit_bytes=vmem * MIB),
            cost_estimate=pl.CostEstimate(flops=flops, bytes_accessed=size, transcendentals=0),
        )(*args)

    return run


def z_shift(value, step):
    return lax.ppermute(value, "z", [(i, (i + step) % 8) for i in range(8)])


def quad_swap(value, flip):
    return lax.ppermute(value, ("yh", "core"), [(i, i ^ flip) for i in range(4)])


def share_shift(value, flip, step):
    pairs = [
        (h * 4 + m, (h ^ flip) * 4 + (m + step) % 4) for h in range(2) for m in range(4)
    ]
    return lax.ppermute(value, ("half", "mp"), pairs)


def quad_place(flip):
    return (lax.axis_index("yh") * 2 + lax.axis_index("core")) ^ flip


def share_place(flip, step):
    return (lax.axis_index("half") ^ flip) * 4 + ((lax.axis_index("mp") + step) & 3)


def columns(place, width):
    return pl.ds(pl.multiple_of(place * width, width if width < 128 else 128), width)


SHARE_MOVES = [(0, 0), (0, 1), (0, 3), (1, 0), (0, 2), (1, 2), (1, 1), (1, 3)]


def split3(value):
    high = value.astype(BF).astype(F32)
    rest = value - high
    mid = rest.astype(BF).astype(F32)
    return high, mid, rest - mid


def message_kernel(queries, keys, values, frames, q_out, kv_out):
    row = jnp.broadcast_to(frames[...].astype(F32), (16, TOK)).astype(BF)
    q_out[0:TOK, :] = queries[...]
    kv_out[0:TOK, :] = keys[...]
    kv_out[TOK : 2 * TOK, :] = values[...]
    for head in range(HEADS):
        at = slice(head * DH, (head + 1) * DH)
        q_out[TOK : TOK + 16, at] = row
        kv_out[2 * TOK : 2 * TOK + 16, at] = row


def attend_kernel(*refs):
    q_refs, kv_refs, far_k, far_v = refs[:4], refs[4:11], refs[11], refs[12]
    outs, stat = refs[13:17], refs[17]
    scale = LOG2E / math.sqrt(DH)
    stat[...] = jnp.zeros_like(stat)
    key_frames = jnp.concatenate(
        [r[2 * TOK : 2 * TOK + 16, 0:TOK].astype(F32)[0:1] for r in kv_refs]
        + [far_v[TOK : TOK + 16, 0:TOK].astype(F32)[0:1]],
        axis=1,
    )
    lane = lax.broadcasted_iota(jnp.int32, (TOK, DH), 1)

    def head_step(head, carry):
        at = pl.ds(pl.multiple_of(head * DH, DH), DH)
        key = jnp.concatenate([r[0:TOK, at] for r in kv_refs] + [far_k[:, at]], axis=0)
        val = jnp.concatenate(
            [r[TOK : 2 * TOK, at] for r in kv_refs] + [far_v[0:TOK, at]], axis=0
        )
        for j in range(4):
            query = q_refs[j][0:TOK, at]
            row = q_refs[j][TOK : TOK + 16, 0:TOK].astype(F32)[0:1]
            turned = jnp.transpose(jnp.broadcast_to(row, (DH, TOK)))
            scores = lax.dot_general(
                query, key, (((1,), (1,)), ((), ())), preferred_element_type=F32
            )
            scores = jnp.where(key_frames <= turned[:, 0:1], scores, -1e30)
            top = jnp.maximum(jnp.max(scores, axis=1, keepdims=True), -1e29)
            weights = jnp.exp2((scores - top) * scale)
            total = jnp.sum(weights, axis=1, keepdims=True)
            mixed = lax.dot_general(
                weights.astype(BF), val, (((1,), (0,)), ((), ())), preferred_element_type=F32
            )
            seen = total > 0.0
            safe = jnp.where(seen, total, 1.0)
            outs[j][:, at] = (mixed / safe).astype(BF)
            level = jnp.where(seen, top * scale + jnp.log2(safe), -1e30)
            high, mid, low = split3(level)
            stat[j] += (
                jnp.where(lane == head, high, 0.0)
                + jnp.where(lane == head + 16, mid, 0.0)
                + jnp.where(lane == head + 32, low, 0.0)
            )
        return carry

    lax.fori_loop(0, HEADS, head_step, 0)
    for j in range(4):
        outs[j][:, HEADS * DH :] = stat[j].astype(BF)


def merged(parts):
    stats = [p[:, HEADS * DH :].astype(F32) for p in parts]
    columns = []
    for head in range(HEADS):
        levels = [
            s[:, head : head + 1] + s[:, head + 16 : head + 17] + s[:, head + 32 : head + 33]
            for s in stats
        ]
        top = functools.reduce(jnp.maximum, levels)
        factors = [jnp.exp2(level - top) for level in levels]
        total = sum(factors[1:], factors[0])
        at = slice(head * DH, (head + 1) * DH)
        mixed = sum(f * p[:, at].astype(F32) for f, p in zip(factors, parts))
        columns.append((mixed / total).astype(BF))
    return jnp.concatenate(columns, axis=1)


def project_kernel(weight, *refs):
    parts, outs, held, sems = refs[:4], refs[4:12], refs[12], refs[13]
    copies = []
    for k in range(8):
        at = columns(share_place(*SHARE_MOVES[k]), 640)
        copies.append(pltpu.make_async_copy(weight.at[:, at], held.at[k], sems.at[k]))
        copies[-1].start()
    attended = merged(parts)
    for k, out in enumerate(outs):
        copies[k].wait()
        out[...] = jnp.dot(attended, held[k], preferred_element_type=F32).astype(BF)


def project(weight, *parts):
    vmem = pl.BlockSpec(memory_space=pltpu.VMEM)
    return pl.pallas_call(
        project_kernel,
        in_specs=[
            pl.BlockSpec(memory_space=pltpu.HBM),
            *[vmem] * 4,
        ],
        out_specs=[vmem] * 8,
        out_shape=[jax.ShapeDtypeStruct((TOK, 640), BF)] * 8,
        scratch_shapes=[pltpu.VMEM((8, 640, 640), BF), pltpu.SemaphoreType.DMA((8,))],
        compiler_params=pltpu.CompilerParams(vmem_limit_bytes=44 * MIB),
        cost_estimate=pl.CostEstimate(flops=840000000, bytes_accessed=9000000, transcendentals=0),
    )(weight, *parts)


def feature_kernel(proj, s_local, s_core, *refs):
    parts, base, outs = refs[:8], refs[8], refs[9:17]
    feature = base[...]
    for part in parts:
        feature = feature + part[...].astype(F32)
    square = jnp.sum(feature * feature, axis=1, keepdims=True)
    turned = jnp.transpose(jnp.broadcast_to(square, (TOK, TOK)))
    high, mid, low = split3(turned[0:16])
    index = lax.broadcasted_iota(jnp.int32, (16, TOK), 0)
    rows = jnp.where(index == 0, high, jnp.where(index == 1, mid, low))
    rows = jnp.concatenate([rows, rows], axis=1).astype(BF)
    narrow = feature.astype(BF)
    for k, out in enumerate(outs):
        at = columns(share_place(*SHARE_MOVES[k]), 256)
        out[0:TOK, :] = jnp.dot(narrow, proj[:, at], preferred_element_type=F32).astype(BF)
        out[TOK : 3 * TOK, :] = (s_local[:, at].astype(F32) + s_core[:, at].astype(F32)).astype(BF)
        out[3 * TOK : 3 * TOK + 16, :] = rows


def away_kernel(*refs):
    total = 0.0
    for part in refs[:8]:
        total = total + part[2 * TOK : 3 * TOK, :].astype(F32)
    refs[8][...] = total.astype(BF)


def error_kernel(inputs, *refs):
    parts, s_y, out = refs[:8], refs[8], refs[9]
    student = inputs[:, columns(share_place(0, 0), 256)].astype(F32) + s_y[...].astype(F32)
    target, rows = 0.0, 0.0
    for part in parts:
        target = target + part[0:TOK, :].astype(F32)
        student = student + part[TOK : 2 * TOK, :].astype(F32)
        rows = rows + part[3 * TOK : 3 * TOK + 16, :].astype(F32)
    square = rows[0:1, 0:TOK] + rows[1:2, 0:TOK] + rows[2:3, 0:TOK]
    column = jnp.transpose(jnp.broadcast_to(square, (TOK, TOK)))[:, 0:1]
    inverse = lax.rsqrt(column * (1.0 / 5120.0) + 1e-6)
    out[...] = ((student - target * inverse) * (1.0 / 64.0)).astype(BF)


def pieces_kernel(w_in, w_out_t, *rest):
    for j, out in enumerate(rest[2:]):
        at = columns(quad_place(j), 256)
        out[0:64, :] = w_in[:, at]
        out[64:128, :] = w_out_t[:, at]


def merge_kernel(p0, p1, p2, p3, *rest):
    out = rest[-1]
    for j, piece in enumerate((p0, p1, p2, p3)):
        begin = pl.multiple_of(quad_place(j) * 64, 64)
        out[pl.ds(begin, 64), :] = piece[0:64, :]
        out[pl.ds(begin + 256, 64), :] = piece[64:128, :]


def student_kernel(x0, x1, x2, x3, weight, *rest):
    slope, hidden_t, local, to_core = rest[-4:]
    pre = jnp.zeros((4 * TOK, 256), F32)
    for z in range(8):
        at = slice(z * 256, (z + 1) * 256)
        rows = jnp.concatenate([x0[:, at], x1[:, at], x2[:, at], x3[:, at]], axis=0)
        pre = pre + jnp.dot(rows, weight[z, 0:256, :], preferred_element_type=F32)
    activated, slope[...] = gelu_parts(pre)
    hidden_t[...] = jnp.transpose(activated).astype(BF)
    hidden = activated.astype(BF)
    for z in range(8):
        at = slice(z * 256, (z + 1) * 256)
        spread = lax.dot_general(
            hidden,
            weight[z, 256:512, :],
            (((1,), (1,)), ((), ())),
            preferred_element_type=F32,
        ).astype(BF)
        for a in range(2):
            local[a * TOK : (a + 1) * TOK, at] = spread[2 * a * TOK : (2 * a + 1) * TOK]
            to_core[a * TOK : (a + 1) * TOK, at] = spread[(2 * a + 1) * TOK : (2 * a + 2) * TOK]


def grad_kernel(*refs):
    weight, slope, hidden_t = refs[0:3]
    x_refs = refs[3:7]
    mine = refs[7:11]
    theirs = refs[11:15]
    outs = refs[15:23]
    rows = refs[23]
    z = lax.axis_index("z")
    for half, blocks in enumerate((mine, theirs)):
        for k, block in enumerate(blocks):
            for flip in range(2):
                cols = columns(share_place(flip, k), 256)
                for a in range(2):
                    source = (a * 2 + flip) * TOK
                    at = (a * 2 + half) * TOK
                    rows[at : at + TOK, cols] = block[source : source + TOK, :]
    back = jnp.zeros((4 * TOK, 256), F32)
    for y in range(8):
        back = back + jnp.dot(
            rows[:, y * 256 : (y + 1) * 256], weight[y, 256:512, :], preferred_element_type=F32
        )
    grad_pre = jnp.transpose(back * slope[...]).astype(BF)
    for k, out in enumerate(outs):
        at = columns((z + Z_MOVES[k]) & 7, 256)
        inputs = jnp.concatenate([r[:, at] for r in x_refs], axis=0)
        out[0:256, :] = jnp.dot(grad_pre, inputs, preferred_element_type=F32).astype(BF)
        out[256:512, :] = jnp.dot(
            hidden_t[...], rows[:, at], preferred_element_type=F32
        ).astype(BF)


def turn_kernel(local, up, down, o0, o1, o2, o3, block):
    total = local[...].astype(F32) + up[...].astype(F32) + down[...].astype(F32)
    block[...] = jnp.transpose(total)
    for j, out in enumerate((o0, o1, o2, o3)):
        at = columns(quad_place(j), 64)
        out[...] = block[at, :].astype(BF)


def final_kernel(p0, p1, p2, p3, grad_in, grad_out_t):
    for j, part in enumerate((p0, p1, p2, p3)):
        at = columns(quad_place(j), 256)
        piece = part[...].astype(F32)
        grad_in[:, at] = piece[:, 0:256]
        grad_out_t[:, at] = piece[:, 256:512]


Z_MOVES = [4, 3, -3, 2, -2, 1, -1, 0]


def gelu_parts(value):
    k = math.sqrt(2.0 / math.pi)
    square = value * value
    bend = jnp.tanh(k * (value + 0.044715 * value * square))
    out = 0.5 * value * (1.0 + bend)
    slope = 0.5 * (1.0 + bend) + 0.5 * value * (1.0 - bend * bend) * k * (
        1.0 + 3.0 * 0.044715 * square
    )
    return out, slope


def per_device(
    queries,
    keys,
    values,
    token_frames,
    frame_actions,
    teacher_resid,
    out_weight,
    action_table,
    projection,
    student_input,
    w_in,
    w_out,
):
    own_q, own_kv = call(
        message_kernel, [((TOK + 16, 640), BF), ((2 * TOK + 16, 640), BF)], fetch=3, vmem=60
    )(queries, keys, values, token_frames.reshape(1, TOK))
    up1, down1 = z_shift(own_kv, 1), z_shift(own_kv, -1)
    pieces = call(pieces_kernel, [((TOK, 256), BF)] * 4, fetch=2, later=2, vmem=44)(
        w_in, w_out.T, up1, down1
    )
    pieces = [pieces[0]] + [quad_swap(pieces[j], j) for j in (1, 2, 3)]
    up2, down2 = z_shift(up1, 1), z_shift(down1, -1)
    q_own, x_own, up2, down2 = lax.optimization_barrier((own_q, student_input, up2, down2))
    q_y = quad_swap(q_own, 2)
    q_c = quad_swap(q_own, 1)
    x_y = quad_swap(x_own, 2)
    up3, down3 = z_shift(up2, 1), z_shift(down2, -1)
    x_own, q_y, q_c, up3, down3 = lax.optimization_barrier((x_own, q_y, q_c, up3, down3))
    far_k, far_v = z_shift(up3[:TOK], 1), z_shift(down3[TOK:], -1)
    q_yc = quad_swap(q_y, 1)
    x_c = quad_swap(x_own, 1)
    x_yc = quad_swap(x_y, 1)
    x_parts = (student_input, x_c, x_y, x_yc)
    (w_block,) = call(merge_kernel, [((512, 256), BF)], later=2, size=500000)(
        *pieces, up3, down3
    )
    w_all = lax.all_gather(w_block, "z", axis=0, tiled=False)

    frame_match = token_frames[:, None] == jnp.arange(24, dtype=jnp.int32)[None, :]
    token_action = jnp.sum(jnp.where(frame_match, frame_actions[None, :], 0), axis=1)
    action_hot = (token_action[:, None] == jnp.arange(64, dtype=jnp.int32)[None, :]).astype(BF)
    base = teacher_resid.astype(F32) + jnp.dot(
        action_hot, action_table, preferred_element_type=F32
    )

    partial = call(
        attend_kernel,
        [((TOK, 768), BF)] * 4,
        [pltpu.VMEM((4, TOK, TOK), F32)],
        fetch=13,
        flops=1400000000,
        size=6000000,
    )(
        own_q, q_c, q_y, q_yc, own_kv, up1, down1, up2, down2, up3, down3, far_k, far_v
    )
    parts = [partial[0]] + [quad_swap(partial[j], j) for j in (1, 2, 3)]
    chunks = project(out_weight, *parts)
    sums = [chunks[0]] + [
        share_shift(c, flip, step) for c, (flip, step) in zip(chunks[1:], SHARE_MOVES[1:])
    ]
    slope, hidden_t, local, to_core = call(
        student_kernel,
        [((512, 256), F32), ((256, 512), BF), ((256, 2048), BF), ((256, 2048), BF)],
        fetch=5,
        later=7,
        vmem=44,
    )(*x_parts, w_all, *sums[1:])
    from_core = quad_swap(to_core, 1)
    chunks = call(
        feature_kernel,
        [((3 * TOK + 16, 256), BF)] * 8,
        fetch=3,
        vmem=44,
        flops=340000000,
        size=5000000,
    )(projection, local, from_core, *sums, base)
    sums = [chunks[0]] + [
        share_shift(c, flip, step) for c, (flip, step) in zip(chunks[1:], SHARE_MOVES[1:])
    ]
    (away,) = call(away_kernel, [((TOK, 256), BF)], flops=1000000, size=800000)(*sums)
    (grad_share,) = call(error_kernel, [((TOK, 256), BF)], fetch=1)(
        student_input, *sums, quad_swap(away, 2)
    )

    def y_move(value, flip_high, flip_low):
        pairs = [
            (h * 2 + y, (h ^ flip_low) * 2 + (y ^ flip_high)) for h in range(2) for y in range(2)
        ]
        return lax.ppermute(value, ("half", "yh"), pairs)

    along_y = jnp.concatenate(
        [grad_share, y_move(grad_share, 0, 1), y_move(grad_share, 1, 0), y_move(grad_share, 1, 1)],
        axis=0,
    )
    mine = [along_y] + [
        lax.ppermute(along_y, "mp", [(i, (i - k) % 4) for i in range(4)]) for k in (1, 2, 3)
    ]
    theirs = [quad_swap(m, 1) for m in mine]
    grads = call(
        grad_kernel,
        [((512, 256), BF)] * 8,
        [pltpu.VMEM((512, 2048), BF)],
        fetch=7,
        vmem=44,
        flops=1700000000,
        size=10000000,
    )(w_all, slope, hidden_t, *x_parts, *mine, *theirs)
    local = dict(zip(Z_MOVES, grads))

    def added(one, two):
        return (one.astype(F32) + two.astype(F32)).astype(BF)

    up = z_shift(local[4][:256], 1)
    down = z_shift(local[4][256:], -1)
    up = z_shift(jnp.concatenate([added(up, local[3][:256]), local[3][256:]], axis=0), 1)
    down = z_shift(jnp.concatenate([local[-3][:256], added(down, local[-3][256:])], axis=0), -1)
    for k in (2, 1):
        up = z_shift(added(up, local[k]), 1)
        down = z_shift(added(down, local[-k]), -1)
    blocks = call(
        turn_kernel,
        [((64, 512), BF)] * 4,
        [pltpu.VMEM((256, 512), F32)],
        flops=1000000,
        size=1000000,
    )(local[0], up, down)
    blocks = [blocks[0]] + [quad_swap(blocks[j], j) for j in (1, 2, 3)]
    grad_in, grad_out_t = call(
        final_kernel, [((64, 1024), F32)] * 2, flops=1000000, size=1000000
    )(*blocks)
    return grad_in, grad_out_t.T


def solution(mesh):
    shape = mesh.devices.shape
    fine = Mesh(
        mesh.devices.reshape(shape[0], 8, 2, 2, shape[2]), ("half", "z", "yh", "core", "mp")
    )
    ctx = ("z", "yh", "core")
    share = ("half", "mp")
    return jax.shard_map(
        per_device,
        mesh=fine,
        in_specs=(
            P(ctx, share),
            P(ctx, share),
            P(ctx, share),
            P(ctx),
            P(),
            P(ctx, share),
            P(share, None),
            P(None, share),
            P(share, None),
            P(ctx, None),
            P(ctx, share),
            P(share, ctx),
        ),
        out_specs=(P(ctx, share), P(share, ctx)),
        check_vma=False,
    )
```

```python
import functools
import math

import jax
import jax.numpy as jnp
from jax import lax
from jax.experimental import pallas as pl
from jax.experimental.pallas import tpu as pltpu
from jax.sharding import Mesh, PartitionSpec as P

DH = 128
HEADS = 5
TOK = 128
BF = jnp.bfloat16
F32 = jnp.float32
LOG2E = 1.4426950408889634
MIB = 1024 * 1024


def call(kernel, outs, scratch=(), fetch=0, later=0, flops=0, size=0, vmem=44):
    def body(*refs):
        held = refs[:fetch]
        tail = refs[len(refs) - fetch - (1 if fetch else 0) :]
        rest = refs[fetch : len(refs) - len(tail)]
        copies = [
            pltpu.make_async_copy(source, target, tail[-1].at[i])
            for i, (source, target) in enumerate(zip(held, tail))
        ]
        for copy in copies:
            copy.start()
        for copy in copies:
            copy.wait()
        kernel(*tail[:fetch], *rest)

    def run(*args):
        count = len(args) - fetch - later
        spaces = [pltpu.HBM] * fetch + [pltpu.VMEM] * count + [pl.ANY] * later
        buffers = [pltpu.VMEM(a.shape, a.dtype) for a in args[:fetch]]
        if fetch:
            buffers.append(pltpu.SemaphoreType.DMA((fetch,)))
        return pl.pallas_call(
            body,
            out_shape=[jax.ShapeDtypeStruct(s, d) for s, d in outs],
            in_specs=[pl.BlockSpec(memory_space=space) for space in spaces],
            out_specs=[pl.BlockSpec(memory_space=pltpu.VMEM) for _ in outs],
            scratch_shapes=list(scratch) + buffers,
            compiler_params=pltpu.CompilerParams(vmem_limit_bytes=vmem * MIB),
            cost_estimate=pl.CostEstimate(flops=flops, bytes_accessed=size, transcendentals=0),
        )(*args)

    return run


def z_shift(value, step):
    return lax.ppermute(value, "z", [(i, (i + step) % 8) for i in range(8)])


def quad_swap(value, flip):
    return lax.ppermute(value, ("yh", "core"), [(i, i ^ flip) for i in range(4)])


def share_shift(value, flip, step):
    pairs = [
        (h * 4 + m, (h ^ flip) * 4 + (m + step) % 4) for h in range(2) for m in range(4)
    ]
    return lax.ppermute(value, ("half", "mp"), pairs)


def quad_place(flip):
    return (lax.axis_index("yh") * 2 + lax.axis_index("core")) ^ flip


def share_place(flip, step):
    return (lax.axis_index("half") ^ flip) * 4 + ((lax.axis_index("mp") + step) & 3)


def columns(place, width):
    return pl.ds(pl.multiple_of(place * width, width if width < 128 else 128), width)


SHARE_MOVES = [(0, 0), (1, 0), (1, 2), (1, 1), (0, 2), (1, 3), (0, 1), (0, 3)]


def split3(value):
    high = value.astype(BF).astype(F32)
    rest = value - high
    mid = rest.astype(BF).astype(F32)
    return high, mid, rest - mid


def message_kernel(queries, keys, values, frames, q_out, kv_out):
    row = jnp.broadcast_to(frames[...].astype(F32), (16, TOK)).astype(BF)
    q_out[0:TOK, :] = queries[...]
    kv_out[0:TOK, :] = keys[...]
    kv_out[TOK : 2 * TOK, :] = values[...]
    for head in range(HEADS):
        at = slice(head * DH, (head + 1) * DH)
        q_out[TOK : TOK + 16, at] = row
        kv_out[2 * TOK : 2 * TOK + 16, at] = row


def attend_kernel(*refs):
    q_refs = (refs[0], *refs[2:5])
    kv_refs, far_k, far_v = (refs[1], *refs[5:11]), refs[11], refs[12]
    outs, stat = refs[13:17], refs[17]
    scale = LOG2E / math.sqrt(DH)
    stat[...] = jnp.zeros_like(stat)
    key_frames = jnp.concatenate(
        [r[2 * TOK : 2 * TOK + 16, 0:TOK].astype(F32)[0:1] for r in kv_refs]
        + [far_v[TOK : TOK + 16, 0:TOK].astype(F32)[0:1]],
        axis=1,
    )
    lane = lax.broadcasted_iota(jnp.int32, (TOK, DH), 1)

    def head_step(head, carry):
        at = pl.ds(pl.multiple_of(head * DH, DH), DH)
        key = jnp.concatenate([r[0:TOK, at] for r in kv_refs] + [far_k[:, at]], axis=0)
        val = jnp.concatenate(
            [r[TOK : 2 * TOK, at] for r in kv_refs] + [far_v[0:TOK, at]], axis=0
        )
        for j in range(4):
            query = q_refs[j][0:TOK, at]
            row = q_refs[j][TOK : TOK + 16, 0:TOK].astype(F32)[0:1]
            turned = jnp.transpose(jnp.broadcast_to(row, (DH, TOK)))
            scores = lax.dot_general(
                query, key, (((1,), (1,)), ((), ())), preferred_element_type=F32
            )
            scores = jnp.where(key_frames <= turned[:, 0:1], scores, -1e30)
            top = jnp.maximum(jnp.max(scores, axis=1, keepdims=True), -1e29)
            weights = jnp.exp2((scores - top) * scale)
            total = jnp.sum(weights, axis=1, keepdims=True)
            mixed = lax.dot_general(
                weights.astype(BF), val, (((1,), (0,)), ((), ())), preferred_element_type=F32
            )
            seen = total > 0.0
            safe = jnp.where(seen, total, 1.0)
            outs[j][:, at] = (mixed / safe).astype(BF)
            level = jnp.where(seen, top * scale + jnp.log2(safe), -1e30)
            high, mid, low = split3(level)
            stat[j] += (
                jnp.where(lane == head, high, 0.0)
                + jnp.where(lane == head + 16, mid, 0.0)
                + jnp.where(lane == head + 32, low, 0.0)
            )
        return carry

    lax.fori_loop(0, HEADS, head_step, 0)
    for j in range(4):
        outs[j][:, HEADS * DH :] = stat[j].astype(BF)


def merged(parts):
    stats = [p[:, HEADS * DH :].astype(F32) for p in parts]
    columns = []
    for head in range(HEADS):
        levels = [
            s[:, head : head + 1] + s[:, head + 16 : head + 17] + s[:, head + 32 : head + 33]
            for s in stats
        ]
        top = functools.reduce(jnp.maximum, levels)
        factors = [jnp.exp2(level - top) for level in levels]
        total = sum(factors[1:], factors[0])
        at = slice(head * DH, (head + 1) * DH)
        mixed = sum(f * p[:, at].astype(F32) for f, p in zip(factors, parts))
        columns.append((mixed / total).astype(BF))
    return jnp.concatenate(columns, axis=1)


def project_kernel(*refs):
    parts, weight, outs = refs[:4], refs[4], refs[5:13]
    attended = merged(parts)
    for k, out in enumerate(outs):
        at = columns(share_place(*SHARE_MOVES[k]), 640)
        out[...] = jnp.dot(attended, weight[:, at], preferred_element_type=F32).astype(BF)


def feature_kernel(proj, s_local, s_core, *refs):
    parts, base, outs = refs[:8], refs[8], refs[9:17]
    feature = base[...]
    for part in parts:
        feature = feature + part[...].astype(F32)
    square = jnp.sum(feature * feature, axis=1, keepdims=True)
    turned = jnp.transpose(jnp.broadcast_to(square, (TOK, TOK)))
    high, mid, low = split3(turned[0:16])
    index = lax.broadcasted_iota(jnp.int32, (16, TOK), 0)
    rows = jnp.where(index == 0, high, jnp.where(index == 1, mid, low))
    rows = jnp.concatenate([rows, rows], axis=1).astype(BF)
    narrow = feature.astype(BF)
    for k, out in enumerate(outs):
        at = columns(share_place(*SHARE_MOVES[k]), 256)
        out[0:TOK, :] = jnp.dot(narrow, proj[:, at], preferred_element_type=F32).astype(BF)
        out[TOK : 3 * TOK, :] = (s_local[:, at].astype(F32) + s_core[:, at].astype(F32)).astype(BF)
        out[3 * TOK : 3 * TOK + 16, :] = rows


def away_kernel(*refs):
    total = 0.0
    for part in refs[:8]:
        total = total + part[2 * TOK : 3 * TOK, :].astype(F32)
    refs[8][...] = total.astype(BF)


def error_kernel(inputs, *refs):
    parts, s_y, out = refs[:8], refs[8], refs[9]
    student = inputs[:, columns(share_place(0, 0), 256)].astype(F32) + s_y[...].astype(F32)
    target, rows = 0.0, 0.0
    for part in parts:
        target = target + part[0:TOK, :].astype(F32)
        student = student + part[TOK : 2 * TOK, :].astype(F32)
        rows = rows + part[3 * TOK : 3 * TOK + 16, :].astype(F32)
    square = rows[0:1, 0:TOK] + rows[1:2, 0:TOK] + rows[2:3, 0:TOK]
    column = jnp.transpose(jnp.broadcast_to(square, (TOK, TOK)))[:, 0:1]
    inverse = lax.rsqrt(column * (1.0 / 5120.0) + 1e-6)
    out[...] = ((student - target * inverse) * (1.0 / 64.0)).astype(BF)


def pieces_kernel(w_in, w_out_t, *rest):
    for j, out in enumerate(rest[2:]):
        at = columns(quad_place(j), 256)
        out[0:64, :] = w_in[:, at]
        out[64:128, :] = w_out_t[:, at]


def merge_kernel(p0, p1, p2, p3, *rest):
    out = rest[-1]
    for j, piece in enumerate((p0, p1, p2, p3)):
        begin = pl.multiple_of(quad_place(j) * 64, 64)
        out[pl.ds(begin, 64), :] = piece[0:64, :]
        out[pl.ds(begin + 256, 64), :] = piece[64:128, :]


def student_kernel(x0, x1, x2, x3, weight, *rest):
    slope, hidden_t, local, to_core = rest[-4:]
    pre = jnp.zeros((4 * TOK, 256), F32)
    for z in range(8):
        at = slice(z * 256, (z + 1) * 256)
        rows = jnp.concatenate([x0[:, at], x1[:, at], x2[:, at], x3[:, at]], axis=0)
        pre = pre + jnp.dot(rows, weight[z, 0:256, :], preferred_element_type=F32)
    activated, slope[...] = gelu_parts(pre)
    hidden_t[...] = jnp.transpose(activated).astype(BF)
    hidden = activated.astype(BF)
    for z in range(8):
        at = slice(z * 256, (z + 1) * 256)
        spread = lax.dot_general(
            hidden,
            weight[z, 256:512, :],
            (((1,), (1,)), ((), ())),
            preferred_element_type=F32,
        ).astype(BF)
        for a in range(2):
            local[a * TOK : (a + 1) * TOK, at] = spread[2 * a * TOK : (2 * a + 1) * TOK]
            to_core[a * TOK : (a + 1) * TOK, at] = spread[(2 * a + 1) * TOK : (2 * a + 2) * TOK]


def grad_kernel(*refs):
    weight, slope, hidden_t = refs[0:3]
    x_refs = refs[3:7]
    mine = refs[7:11]
    theirs = refs[11:15]
    in_outs, out_outs = refs[15:23], refs[23:31]
    rows = refs[31]
    z = lax.axis_index("z")
    for half, blocks in enumerate((mine, theirs)):
        for k, block in enumerate(blocks):
            for flip in range(2):
                cols = columns(share_place(flip, k), 256)
                for a in range(2):
                    source = (a * 2 + flip) * TOK
                    at = (a * 2 + half) * TOK
                    rows[at : at + TOK, cols] = block[source : source + TOK, :]
    back = jnp.zeros((4 * TOK, 256), F32)
    for y in range(8):
        back = back + jnp.dot(
            rows[:, y * 256 : (y + 1) * 256], weight[y, 256:512, :], preferred_element_type=F32
        )
    grad_pre = jnp.transpose(back * slope[...]).astype(BF)
    for k in range(8):
        at = columns((z + Z_MOVES[k]) & 7, 256)
        inputs = jnp.concatenate([r[:, at] for r in x_refs], axis=0)
        in_outs[k][...] = jnp.dot(grad_pre, inputs, preferred_element_type=F32).astype(BF)
        out_outs[k][...] = jnp.dot(
            hidden_t[...], rows[:, at], preferred_element_type=F32
        ).astype(BF)


def turn_kernel(a0, a1, a2, b0, b1, b2, o0, o1, o2, o3, block):
    for half, (one, two, three) in enumerate(((a0, a1, a2), (b0, b1, b2))):
        total = one[...].astype(F32) + two[...].astype(F32) + three[...].astype(F32)
        block[:, half * 256 : (half + 1) * 256] = jnp.transpose(total)
    for j, out in enumerate((o0, o1, o2, o3)):
        at = columns(quad_place(j), 64)
        out[...] = block[at, :].astype(BF)


def final_kernel(p0, p1, p2, p3, grad_in, grad_out_t):
    for j, part in enumerate((p0, p1, p2, p3)):
        at = columns(quad_place(j), 256)
        piece = part[...].astype(F32)
        grad_in[:, at] = piece[:, 0:256]
        grad_out_t[:, at] = piece[:, 256:512]


Z_MOVES = [4, 3, -3, 2, -2, 1, -1, 0]


def gelu_parts(value):
    k = math.sqrt(2.0 / math.pi)
    square = value * value
    bend = jnp.tanh(k * (value + 0.044715 * value * square))
    out = 0.5 * value * (1.0 + bend)
    slope = 0.5 * (1.0 + bend) + 0.5 * value * (1.0 - bend * bend) * k * (
        1.0 + 3.0 * 0.044715 * square
    )
    return out, slope


def per_device(
    queries,
    keys,
    values,
    token_frames,
    frame_actions,
    teacher_resid,
    out_weight,
    action_table,
    projection,
    student_input,
    w_in,
    w_out,
):
    own_q, own_kv = call(
        message_kernel, [((TOK + 16, 640), BF), ((2 * TOK + 16, 640), BF)], fetch=3, vmem=60
    )(queries, keys, values, token_frames.reshape(1, TOK))
    up1, down1 = z_shift(own_kv, 1), z_shift(own_kv, -1)
    q_y = quad_swap(own_q, 2)
    q_c = quad_swap(own_q, 1)
    q_y, q_c, up1, down1 = lax.optimization_barrier((q_y, q_c, up1, down1))
    up2, down2 = z_shift(up1, 1), z_shift(down1, -1)
    pieces = call(pieces_kernel, [((TOK, 256), BF)] * 4, fetch=2, later=2)(
        w_in, w_out.T, up1, down1
    )
    pieces = [pieces[0]] + [quad_swap(pieces[j], j) for j in (1, 2, 3)]
    p1, p2, p3, up2, down2 = lax.optimization_barrier((*pieces[1:], up2, down2))
    up3, down3 = z_shift(up2, 1), z_shift(down2, -1)
    x_own, q_y = lax.optimization_barrier((student_input, q_y, up2))[:2]
    x_y = quad_swap(x_own, 2)
    q_yc = quad_swap(q_y, 1)
    x_c = quad_swap(x_own, 1)
    q_yc, x_c, up3, down3 = lax.optimization_barrier((q_yc, x_c, up3, down3))
    far_k, far_v = z_shift(up3[:TOK], 1), z_shift(down3[TOK:], -1)
    far_k, far_v, x_y = lax.optimization_barrier((far_k, far_v, x_y))

    frame_match = token_frames[:, None] == jnp.arange(24, dtype=jnp.int32)[None, :]
    token_action = jnp.sum(jnp.where(frame_match, frame_actions[None, :], 0), axis=1)
    action_hot = (token_action[:, None] == jnp.arange(64, dtype=jnp.int32)[None, :]).astype(BF)
    base = teacher_resid.astype(F32) + jnp.dot(
        action_hot, action_table, preferred_element_type=F32
    )

    partial = call(
        attend_kernel,
        [((TOK, 768), BF)] * 4,
        [pltpu.VMEM((4, TOK, TOK), F32)],
        fetch=2,
        flops=1400000000,
        size=6000000,
    )(
        own_q, own_kv, q_c, q_y, q_yc, up1, down1, up2, down2, up3, down3, far_k, far_v
    )
    (w_block,) = call(merge_kernel, [((512, 256), BF)], later=1, size=500000)(
        pieces[0], p1, p2, p3, partial[0]
    )
    w_all = lax.all_gather(w_block, "z", axis=0, tiled=False)
    x_yc = quad_swap(x_y, 1)
    x_parts = (student_input, x_c, x_y, x_yc)
    parts = [partial[0]] + [quad_swap(partial[j], j) for j in (1, 2, 3)]
    chunks = call(
        project_kernel, [((TOK, 640), BF)] * 8, flops=840000000, size=9000000
    )(*parts, out_weight)
    sums = [chunks[0]] + [
        share_shift(c, flip, step) for c, (flip, step) in zip(chunks[1:], SHARE_MOVES[1:])
    ]
    slope, hidden_t, local, to_core = call(
        student_kernel,
        [((512, 256), F32), ((256, 512), BF), ((256, 2048), BF), ((256, 2048), BF)],
        fetch=5,
        later=6,
    )(*x_parts, w_all, *sums[1:7])
    from_core = quad_swap(to_core, 1)
    chunks = call(
        feature_kernel,
        [((3 * TOK + 16, 256), BF)] * 8,
        fetch=3,
        vmem=44,
        flops=340000000,
        size=5000000,
    )(projection, local, from_core, *sums, base)
    sums = [chunks[0]] + [
        share_shift(c, flip, step) for c, (flip, step) in zip(chunks[1:], SHARE_MOVES[1:])
    ]
    (away,) = call(away_kernel, [((TOK, 256), BF)], flops=1000000, size=800000)(*sums)
    (grad_share,) = call(error_kernel, [((TOK, 256), BF)], fetch=1)(
        student_input, *sums, quad_swap(away, 2)
    )

    def y_move(value, flip_high, flip_low):
        pairs = [
            (h * 2 + y, (h ^ flip_low) * 2 + (y ^ flip_high)) for h in range(2) for y in range(2)
        ]
        return lax.ppermute(value, ("half", "yh"), pairs)

    along_y = jnp.concatenate(
        [grad_share, y_move(grad_share, 0, 1), y_move(grad_share, 1, 0), y_move(grad_share, 1, 1)],
        axis=0,
    )
    mine = [along_y] + [
        lax.ppermute(along_y, "mp", [(i, (i - k) % 4) for i in range(4)]) for k in (1, 2, 3)
    ]
    theirs = [quad_swap(m, 1) for m in mine]
    grads = call(
        grad_kernel,
        [((256, 256), BF)] * 16,
        [pltpu.VMEM((512, 2048), BF)],
        fetch=7,
        vmem=44,
        flops=1700000000,
        size=10000000,
    )(w_all, slope, hidden_t, *x_parts, *mine, *theirs)
    grad_a, grad_b = dict(zip(Z_MOVES, grads[:8])), dict(zip(Z_MOVES, grads[8:]))

    def added(one, two):
        return (one.astype(F32) + two.astype(F32)).astype(BF)

    up_a, down_b = z_shift(grad_a[4], 1), z_shift(grad_b[4], -1)
    up_b, down_a = z_shift(grad_b[3], 1), z_shift(grad_a[-3], -1)
    up_a, down_b = z_shift(added(up_a, grad_a[3]), 1), z_shift(added(down_b, grad_b[-3]), -1)
    for k in (2, 1):
        up_b = z_shift(added(up_b, grad_b[k]), 1)
        down_a = z_shift(added(down_a, grad_a[-k]), -1)
        up_a = z_shift(added(up_a, grad_a[k]), 1)
        down_b = z_shift(added(down_b, grad_b[-k]), -1)
    blocks = call(
        turn_kernel,
        [((64, 512), BF)] * 4,
        [pltpu.VMEM((256, 512), F32)],
        flops=1000000,
        size=1000000,
    )(grad_a[0], up_a, down_a, grad_b[0], up_b, down_b)
    blocks = [blocks[0]] + [quad_swap(blocks[j], j) for j in (1, 2, 3)]
    grad_in, grad_out_t = call(
        final_kernel, [((64, 1024), F32)] * 2, flops=1000000, size=1000000
    )(*blocks)
    return grad_in, grad_out_t.T


def solution(mesh):
    shape = mesh.devices.shape
    fine = Mesh(
        mesh.devices.reshape(shape[0], 8, 2, 2, shape[2]), ("half", "z", "yh", "core", "mp")
    )
    ctx = ("z", "yh", "core")
    share = ("half", "mp")
    return jax.shard_map(
        per_device,
        mesh=fine,
        in_specs=(
            P(ctx, share),
            P(ctx, share),
            P(ctx, share),
            P(ctx),
            P(),
            P(ctx, share),
            P(share, None),
            P(None, share),
            P(share, None),
            P(ctx, None),
            P(ctx, share),
            P(share, ctx),
        ),
        out_specs=(P(ctx, share), P(share, ctx)),
        check_vma=False,
    )
```

```python
import functools
import math

import jax
import jax.numpy as jnp
from jax import lax
from jax.experimental import pallas as pl
from jax.experimental.pallas import tpu as pltpu
from jax.sharding import Mesh, PartitionSpec as P

DH = 128
HEADS = 5
TOK = 128
BF = jnp.bfloat16
F32 = jnp.float32
LOG2E = 1.4426950408889634
MIB = 1024 * 1024


def call(kernel, outs, scratch=(), fetch=0, later=0, flops=0, size=0, vmem=44):
    def body(*refs):
        held = refs[:fetch]
        tail = refs[len(refs) - fetch - (1 if fetch else 0) :]
        rest = refs[fetch : len(refs) - len(tail)]
        copies = [
            pltpu.make_async_copy(source, target, tail[-1].at[i])
            for i, (source, target) in enumerate(zip(held, tail))
        ]
        for copy in copies:
            copy.start()
        for copy in copies:
            copy.wait()
        kernel(*tail[:fetch], *rest)

    def run(*args):
        count = len(args) - fetch - later
        spaces = [pltpu.HBM] * fetch + [pltpu.VMEM] * count + [pl.ANY] * later
        buffers = [pltpu.VMEM(a.shape, a.dtype) for a in args[:fetch]]
        if fetch:
            buffers.append(pltpu.SemaphoreType.DMA((fetch,)))
        return pl.pallas_call(
            body,
            out_shape=[jax.ShapeDtypeStruct(s, d) for s, d in outs],
            in_specs=[pl.BlockSpec(memory_space=space) for space in spaces],
            out_specs=[pl.BlockSpec(memory_space=pltpu.VMEM) for _ in outs],
            scratch_shapes=list(scratch) + buffers,
            compiler_params=pltpu.CompilerParams(vmem_limit_bytes=vmem * MIB),
            cost_estimate=pl.CostEstimate(flops=flops, bytes_accessed=size, transcendentals=0),
        )(*args)

    return run


def z_shift(value, step):
    return lax.ppermute(value, "z", [(i, (i + step) % 8) for i in range(8)])


def quad_swap(value, flip):
    return lax.ppermute(value, ("yh", "core"), [(i, i ^ flip) for i in range(4)])


def share_shift(value, flip, step):
    pairs = [
        (h * 4 + m, (h ^ flip) * 4 + (m + step) % 4) for h in range(2) for m in range(4)
    ]
    return lax.ppermute(value, ("half", "mp"), pairs)


def quad_place(flip):
    return (lax.axis_index("yh") * 2 + lax.axis_index("core")) ^ flip


def share_place(flip, step):
    return (lax.axis_index("half") ^ flip) * 4 + ((lax.axis_index("mp") + step) & 3)


def columns(place, width):
    return pl.ds(pl.multiple_of(place * width, width if width < 128 else 128), width)


SHARE_MOVES = [(0, 0), (1, 0), (1, 2), (1, 1), (0, 2), (1, 3), (0, 1), (0, 3)]


def split3(value):
    high = value.astype(BF).astype(F32)
    rest = value - high
    mid = rest.astype(BF).astype(F32)
    return high, mid, rest - mid


def message_kernel(queries, keys, values, inputs, w_in, w_out_t, frames, *outs):
    kv_out, core_out, y_out, piece_out = outs
    row = jnp.broadcast_to(frames[...].astype(F32), (16, TOK)).astype(BF)
    kv_out[0:TOK, :] = keys[...]
    kv_out[TOK : 2 * TOK, :] = values[...]
    for head in range(HEADS):
        kv_out[2 * TOK : 2 * TOK + 16, head * DH : (head + 1) * DH] = row
    for out in (core_out, y_out):
        out[...] = jnp.zeros_like(out)
        out[0:TOK, 0 : HEADS * DH] = queries[...]
        out[TOK : TOK + 16, 0:TOK] = row
    core_out[0:TOK, 896:2944] = inputs[...]
    places = ((piece_out, 0, 0), (core_out, 640, 1), (y_out, 640, 3), (y_out, 896, 2))
    for out, begin, flip in places:
        at = columns(quad_place(flip), 256)
        out[0:64, begin : begin + 256] = w_in[:, at]
        out[64:128, begin : begin + 256] = w_out_t[:, at]


def attend_kernel(*refs):
    q_refs = (refs[0], *refs[2:5])
    kv_refs, far_k, far_v = (refs[1], *refs[5:11]), refs[11], refs[12]
    outs, stat = refs[13:17], refs[17]
    scale = LOG2E / math.sqrt(DH)
    stat[...] = jnp.zeros_like(stat)
    key_frames = jnp.concatenate(
        [r[2 * TOK : 2 * TOK + 16, 0:TOK].astype(F32)[0:1] for r in kv_refs]
        + [far_v[TOK : TOK + 16, 0:TOK].astype(F32)[0:1]],
        axis=1,
    )
    lane = lax.broadcasted_iota(jnp.int32, (TOK, DH), 1)

    def head_step(head, carry):
        at = pl.ds(pl.multiple_of(head * DH, DH), DH)
        key = jnp.concatenate([r[0:TOK, at] for r in kv_refs] + [far_k[:, at]], axis=0)
        val = jnp.concatenate(
            [r[TOK : 2 * TOK, at] for r in kv_refs] + [far_v[0:TOK, at]], axis=0
        )
        for j in range(4):
            query = q_refs[j][0:TOK, at]
            row = q_refs[j][TOK : TOK + 16, 0:TOK].astype(F32)[0:1]
            turned = jnp.transpose(jnp.broadcast_to(row, (DH, TOK)))
            scores = lax.dot_general(
                query, key, (((1,), (1,)), ((), ())), preferred_element_type=F32
            )
            scores = jnp.where(key_frames <= turned[:, 0:1], scores, -1e30)
            top = jnp.maximum(jnp.max(scores, axis=1, keepdims=True), -1e29)
            weights = jnp.exp2((scores - top) * scale)
            total = jnp.sum(weights, axis=1, keepdims=True)
            mixed = lax.dot_general(
                weights.astype(BF), val, (((1,), (0,)), ((), ())), preferred_element_type=F32
            )
            seen = total > 0.0
            safe = jnp.where(seen, total, 1.0)
            outs[j][:, at] = (mixed / safe).astype(BF)
            level = jnp.where(seen, top * scale + jnp.log2(safe), -1e30)
            high, mid, low = split3(level)
            stat[j] += (
                jnp.where(lane == head, high, 0.0)
                + jnp.where(lane == head + 16, mid, 0.0)
                + jnp.where(lane == head + 32, low, 0.0)
            )
        return carry

    lax.fori_loop(0, HEADS, head_step, 0)
    for j in range(4):
        outs[j][:, HEADS * DH :] = stat[j].astype(BF)


def merged(parts):
    stats = [p[:, HEADS * DH :].astype(F32) for p in parts]
    columns = []
    for head in range(HEADS):
        levels = [
            s[:, head : head + 1] + s[:, head + 16 : head + 17] + s[:, head + 32 : head + 33]
            for s in stats
        ]
        top = functools.reduce(jnp.maximum, levels)
        factors = [jnp.exp2(level - top) for level in levels]
        total = sum(factors[1:], factors[0])
        at = slice(head * DH, (head + 1) * DH)
        mixed = sum(f * p[:, at].astype(F32) for f, p in zip(factors, parts))
        columns.append((mixed / total).astype(BF))
    return jnp.concatenate(columns, axis=1)


def project_kernel(weight, *refs):
    parts, outs, held, sems = refs[:4], refs[4:12], refs[12], refs[13]
    copies = []
    for k in range(8):
        at = columns(share_place(*SHARE_MOVES[k]), 640)
        copies.append(pltpu.make_async_copy(weight.at[:, at], held.at[k], sems.at[k]))
        copies[-1].start()
    attended = merged(parts)
    for k, out in enumerate(outs):
        copies[k].wait()
        out[...] = jnp.dot(attended, held[k], preferred_element_type=F32).astype(BF)


def project(weight, *parts):
    vmem = pl.BlockSpec(memory_space=pltpu.VMEM)
    return pl.pallas_call(
        project_kernel,
        in_specs=[pl.BlockSpec(memory_space=pltpu.HBM), *[vmem] * 4],
        out_specs=[vmem] * 8,
        out_shape=[jax.ShapeDtypeStruct((TOK, 640), BF)] * 8,
        scratch_shapes=[pltpu.VMEM((8, 640, 640), BF), pltpu.SemaphoreType.DMA((8,))],
        compiler_params=pltpu.CompilerParams(vmem_limit_bytes=50 * MIB),
        cost_estimate=pl.CostEstimate(flops=840000000, bytes_accessed=9000000, transcendentals=0),
    )(weight, *parts)


def feature_kernel(proj, s_local, s_core, s_y, *refs):
    parts, base, outs = refs[:8], refs[8], refs[9:17]
    feature = base[...]
    for part in parts:
        feature = feature + part[...].astype(F32)
    square = jnp.sum(feature * feature, axis=1, keepdims=True)
    turned = jnp.transpose(jnp.broadcast_to(square, (TOK, TOK)))
    high, mid, low = split3(turned[0:16])
    index = lax.broadcasted_iota(jnp.int32, (16, TOK), 0)
    rows = jnp.where(index == 0, high, jnp.where(index == 1, mid, low))
    rows = jnp.concatenate([rows, rows], axis=1).astype(BF)
    narrow = feature.astype(BF)
    for k, out in enumerate(outs):
        at = columns(share_place(*SHARE_MOVES[k]), 256)
        out[0:TOK, :] = jnp.dot(narrow, proj[:, at], preferred_element_type=F32).astype(BF)
        near = s_local[0:TOK, at].astype(F32) + s_core[0:TOK, at].astype(F32)
        out[TOK : 2 * TOK, :] = (near + s_y[:, at].astype(F32)).astype(BF)
        out[2 * TOK : 2 * TOK + 16, :] = rows


def away_kernel(local, got, out):
    out[...] = (local[TOK:, :].astype(F32) + got[TOK:, :].astype(F32)).astype(BF)


def error_kernel(inputs, *refs):
    parts, out = refs[:8], refs[8]
    student = inputs[:, columns(share_place(0, 0), 256)].astype(F32)
    target, rows = 0.0, 0.0
    for part in parts:
        target = target + part[0:TOK, :].astype(F32)
        student = student + part[TOK : 2 * TOK, :].astype(F32)
        rows = rows + part[2 * TOK : 2 * TOK + 16, :].astype(F32)
    square = rows[0:1, 0:TOK] + rows[1:2, 0:TOK] + rows[2:3, 0:TOK]
    column = jnp.transpose(jnp.broadcast_to(square, (TOK, TOK)))[:, 0:1]
    inverse = lax.rsqrt(column * (1.0 / 5120.0) + 1e-6)
    out[...] = ((student - target * inverse) * (1.0 / 64.0)).astype(BF)


def merge_kernel(own, from_core, from_y, from_both, out):
    blocks = ((own, 0), (from_core, 640), (from_y, 896), (from_both, 640))
    for j, (piece, at) in enumerate(blocks):
        begin = pl.multiple_of(quad_place(j) * 64, 64)
        out[pl.ds(begin, 64), :] = piece[0:64, at : at + 256]
        out[pl.ds(begin + 256, 64), :] = piece[64:128, at : at + 256]


def student_kernel(x0, x1, x2, x3, weight, *rest):
    slope, hidden_t, local, to_core = rest[-4:]
    pre = jnp.zeros((4 * TOK, 256), F32)
    for z in range(8):
        at = slice(z * 256, (z + 1) * 256)
        shifted = slice(z * 256 + 896, (z + 1) * 256 + 896)
        rows = jnp.concatenate([x0[:, at], x1[0:TOK, shifted], x2[:, at], x3[:, at]], axis=0)
        pre = pre + jnp.dot(rows, weight[z, 0:256, :], preferred_element_type=F32)
    activated, slope[...] = gelu_parts(pre)
    hidden_t[...] = jnp.transpose(activated).astype(BF)
    hidden = activated.astype(BF)
    for z in range(8):
        at = slice(z * 256, (z + 1) * 256)
        spread = lax.dot_general(
            hidden,
            weight[z, 256:512, :],
            (((1,), (1,)), ((), ())),
            preferred_element_type=F32,
        ).astype(BF)
        for a in range(2):
            local[a * TOK : (a + 1) * TOK, at] = spread[2 * a * TOK : (2 * a + 1) * TOK]
            to_core[a * TOK : (a + 1) * TOK, at] = spread[(2 * a + 1) * TOK : (2 * a + 2) * TOK]


def grad_kernel(*refs):
    weight, slope, hidden_t = refs[0:3]
    x_refs = refs[3:7]
    mine = refs[7:11]
    theirs = refs[11:15]
    in_outs, out_outs = refs[15:23], refs[23:31]
    rows = refs[31]
    z = lax.axis_index("z")
    for half, blocks in enumerate((mine, theirs)):
        for k, block in enumerate(blocks):
            for flip in range(2):
                cols = columns(share_place(flip, k), 256)
                for a in range(2):
                    source = (a * 2 + flip) * TOK
                    at = (a * 2 + half) * TOK
                    rows[at : at + TOK, cols] = block[source : source + TOK, :]
    back = jnp.zeros((4 * TOK, 256), F32)
    for y in range(8):
        back = back + jnp.dot(
            rows[:, y * 256 : (y + 1) * 256], weight[y, 256:512, :], preferred_element_type=F32
        )
    grad_pre = jnp.transpose(back * slope[...]).astype(BF)
    for k in range(8):
        at = columns((z + Z_MOVES[k]) & 7, 256)
        shifted = columns(((z + Z_MOVES[k]) & 7) * 2 + 7, 128)
        shifted = pl.ds(shifted.start, 256)
        x0, x1, x2, x3 = x_refs
        inputs = jnp.concatenate([x0[:, at], x1[0:TOK, shifted], x2[:, at], x3[:, at]], axis=0)
        in_outs[k][...] = jnp.dot(grad_pre, inputs, preferred_element_type=F32).astype(BF)
        out_outs[k][...] = jnp.dot(
            hidden_t[...], rows[:, at], preferred_element_type=F32
        ).astype(BF)


def turn_kernel(a0, a1, a2, b0, b1, b2, o0, o1, o2, o3, block):
    for half, (one, two, three) in enumerate(((a0, a1, a2), (b0, b1, b2))):
        total = one[...].astype(F32) + two[...].astype(F32) + three[...].astype(F32)
        block[:, half * 256 : (half + 1) * 256] = jnp.transpose(total)
    for j, out in enumerate((o0, o1, o2, o3)):
        at = columns(quad_place(j), 64)
        out[...] = block[at, :].astype(BF)


def final_kernel(p0, p1, p2, p3, grad_in, grad_out_t):
    for j, part in enumerate((p0, p1, p2, p3)):
        at = columns(quad_place(j), 256)
        piece = part[...].astype(F32)
        grad_in[:, at] = piece[:, 0:256]
        grad_out_t[:, at] = piece[:, 256:512]


Z_MOVES = [4, 3, -3, 2, -2, 1, -1, 0]


def gelu_parts(value):
    k = math.sqrt(2.0 / math.pi)
    square = value * value
    bend = jnp.tanh(k * (value + 0.044715 * value * square))
    out = 0.5 * value * (1.0 + bend)
    slope = 0.5 * (1.0 + bend) + 0.5 * value * (1.0 - bend * bend) * k * (
        1.0 + 3.0 * 0.044715 * square
    )
    return out, slope


def per_device(
    queries,
    keys,
    values,
    token_frames,
    frame_actions,
    teacher_resid,
    out_weight,
    action_table,
    projection,
    student_input,
    w_in,
    w_out,
):
    own_kv, to_core, to_y, own_piece = call(
        message_kernel,
        [
            ((2 * TOK + 16, 640), BF),
            ((TOK + 16, 2944), BF),
            ((TOK + 16, 1152), BF),
            ((TOK, 256), BF),
        ],
        fetch=6,
        vmem=60,
    )(queries, keys, values, student_input, w_in, w_out.T, token_frames.reshape(1, TOK))
    up1, down1 = z_shift(own_kv, 1), z_shift(own_kv, -1)
    from_y = quad_swap(to_y, 2)
    from_core = quad_swap(to_core, 1)
    from_y, from_core, up1, down1 = lax.optimization_barrier((from_y, from_core, up1, down1))
    up2, down2 = z_shift(up1, 1), z_shift(down1, -1)
    from_both = quad_swap(from_y, 1)
    from_both, up2, down2 = lax.optimization_barrier((from_both, up2, down2))
    (w_block,) = call(merge_kernel, [((512, 256), BF)], size=500000)(
        own_piece, from_core, from_y, from_both
    )
    w_all = lax.all_gather(w_block, "z", axis=0, tiled=False)
    up3, down3 = z_shift(up2, 1), z_shift(down2, -1)
    x_own = lax.optimization_barrier((student_input, up2))[0]
    x_y = quad_swap(x_own, 2)
    far_k, far_v = z_shift(up3[:TOK], 1), z_shift(down3[TOK:], -1)
    far_k, far_v, x_y = lax.optimization_barrier((far_k, far_v, x_y))

    frame_match = token_frames[:, None] == jnp.arange(24, dtype=jnp.int32)[None, :]
    token_action = jnp.sum(jnp.where(frame_match, frame_actions[None, :], 0), axis=1)
    action_hot = (token_action[:, None] == jnp.arange(64, dtype=jnp.int32)[None, :]).astype(BF)
    base = teacher_resid.astype(F32) + jnp.dot(
        action_hot, action_table, preferred_element_type=F32
    )

    partial = call(
        attend_kernel,
        [((TOK, 768), BF)] * 4,
        [pltpu.VMEM((4, TOK, TOK), F32)],
        fetch=2,
        flops=1400000000,
        size=6000000,
    )(
        to_core, own_kv, from_core, from_y, from_both,
        up1, down1, up2, down2, up3, down3, far_k, far_v,
    )
    x_parts = (student_input, from_core, x_y, quad_swap(x_y, 1))
    parts = [partial[0]] + [quad_swap(partial[j], j) for j in (1, 2, 3)]
    slope, hidden_t, local, local_core = call(
        student_kernel,
        [((512, 256), F32), ((256, 512), BF), ((256, 2048), BF), ((256, 2048), BF)],
        fetch=5,
        later=2,
    )(*x_parts, w_all, parts[2], parts[3])
    got_core = quad_swap(local_core, 1)
    (away,) = call(away_kernel, [((TOK, 2048), BF)])(local, got_core)
    got_y = quad_swap(away, 2)
    chunks = project(out_weight, *parts)
    sums = [chunks[0]] + [
        share_shift(c, flip, step) for c, (flip, step) in zip(chunks[1:], SHARE_MOVES[1:])
    ]
    chunks = call(
        feature_kernel,
        [((2 * TOK + 16, 256), BF)] * 8,
        fetch=4,
        vmem=44,
        flops=340000000,
        size=5000000,
    )(projection, local, got_core, got_y, *sums, base)
    sums = [chunks[0]] + [
        share_shift(c, flip, step) for c, (flip, step) in zip(chunks[1:], SHARE_MOVES[1:])
    ]
    (grad_share,) = call(error_kernel, [((TOK, 256), BF)], fetch=1)(
        student_input, *sums
    )

    def y_move(value, flip_high, flip_low):
        pairs = [
            (h * 2 + y, (h ^ flip_low) * 2 + (y ^ flip_high)) for h in range(2) for y in range(2)
        ]
        return lax.ppermute(value, ("half", "yh"), pairs)

    along_y = jnp.concatenate(
        [grad_share, y_move(grad_share, 0, 1), y_move(grad_share, 1, 0), y_move(grad_share, 1, 1)],
        axis=0,
    )
    mine = [along_y] + [
        lax.ppermute(along_y, "mp", [(i, (i - k) % 4) for i in range(4)]) for k in (1, 2, 3)
    ]
    theirs = [quad_swap(m, 1) for m in mine]
    grads = call(
        grad_kernel,
        [((256, 256), BF)] * 16,
        [pltpu.VMEM((512, 2048), BF)],
        fetch=7,
        vmem=44,
        flops=1700000000,
        size=10000000,
    )(w_all, slope, hidden_t, *x_parts, *mine, *theirs)
    grad_a, grad_b = dict(zip(Z_MOVES, grads[:8])), dict(zip(Z_MOVES, grads[8:]))

    def added(one, two):
        return (one.astype(F32) + two.astype(F32)).astype(BF)

    up_a, down_b = z_shift(grad_a[4], 1), z_shift(grad_b[4], -1)
    up_b, down_a = z_shift(grad_b[3], 1), z_shift(grad_a[-3], -1)
    up_a, down_b = z_shift(added(up_a, grad_a[3]), 1), z_shift(added(down_b, grad_b[-3]), -1)
    for k in (2, 1):
        up_b = z_shift(added(up_b, grad_b[k]), 1)
        down_a = z_shift(added(down_a, grad_a[-k]), -1)
        up_a = z_shift(added(up_a, grad_a[k]), 1)
        down_b = z_shift(added(down_b, grad_b[-k]), -1)
    blocks = call(
        turn_kernel,
        [((64, 512), BF)] * 4,
        [pltpu.VMEM((256, 512), F32)],
        flops=1000000,
        size=1000000,
    )(grad_a[0], up_a, down_a, grad_b[0], up_b, down_b)
    blocks = [blocks[0]] + [quad_swap(blocks[j], j) for j in (1, 2, 3)]
    grad_in, grad_out_t = call(
        final_kernel, [((64, 1024), F32)] * 2, flops=1000000, size=1000000
    )(*blocks)
    return grad_in, grad_out_t.T


def solution(mesh):
    shape = mesh.devices.shape
    fine = Mesh(
        mesh.devices.reshape(shape[0], 8, 2, 2, shape[2]), ("half", "z", "yh", "core", "mp")
    )
    ctx = ("z", "yh", "core")
    share = ("half", "mp")
    return jax.shard_map(
        per_device,
        mesh=fine,
        in_specs=(
            P(ctx, share),
            P(ctx, share),
            P(ctx, share),
            P(ctx),
            P(),
            P(ctx, share),
            P(share, None),
            P(None, share),
            P(share, None),
            P(ctx, None),
            P(ctx, share),
            P(share, ctx),
        ),
        out_specs=(P(ctx, share), P(share, ctx)),
        check_vma=False,
    )
```

```python
import functools
import math

import jax
import jax.numpy as jnp
from jax import lax
from jax.experimental import pallas as pl
from jax.experimental.pallas import tpu as pltpu
from jax.sharding import Mesh, PartitionSpec as P

DH = 128
HEADS = 5
TOK = 128
BF = jnp.bfloat16
F32 = jnp.float32
LOG2E = 1.4426950408889634
MIB = 1024 * 1024


def call(kernel, outs, scratch=(), fetch=0, later=0, flops=0, size=0, vmem=44):
    def body(*refs):
        held = refs[:fetch]
        tail = refs[len(refs) - fetch - (1 if fetch else 0) :]
        rest = refs[fetch : len(refs) - len(tail)]
        copies = [
            pltpu.make_async_copy(source, target, tail[-1].at[i])
            for i, (source, target) in enumerate(zip(held, tail))
        ]
        for copy in copies:
            copy.start()
        for copy in copies:
            copy.wait()
        kernel(*tail[:fetch], *rest)

    def run(*args):
        count = len(args) - fetch - later
        spaces = [pltpu.HBM] * fetch + [pltpu.VMEM] * count + [pl.ANY] * later
        buffers = [pltpu.VMEM(a.shape, a.dtype) for a in args[:fetch]]
        if fetch:
            buffers.append(pltpu.SemaphoreType.DMA((fetch,)))
        return pl.pallas_call(
            body,
            out_shape=[jax.ShapeDtypeStruct(s, d) for s, d in outs],
            in_specs=[pl.BlockSpec(memory_space=space) for space in spaces],
            out_specs=[pl.BlockSpec(memory_space=pltpu.VMEM) for _ in outs],
            scratch_shapes=list(scratch) + buffers,
            compiler_params=pltpu.CompilerParams(vmem_limit_bytes=vmem * MIB),
            cost_estimate=pl.CostEstimate(flops=flops, bytes_accessed=size, transcendentals=0),
        )(*args)

    return run


def z_shift(value, step):
    return lax.ppermute(value, "z", [(i, (i + step) % 8) for i in range(8)])


def quad_swap(value, flip):
    return lax.ppermute(value, ("yh", "core"), [(i, i ^ flip) for i in range(4)])


def share_shift(value, flip, step):
    pairs = [
        (h * 4 + m, (h ^ flip) * 4 + (m + step) % 4) for h in range(2) for m in range(4)
    ]
    return lax.ppermute(value, ("half", "mp"), pairs)


def quad_place(flip):
    return (lax.axis_index("yh") * 2 + lax.axis_index("core")) ^ flip


def share_place(flip, step):
    return (lax.axis_index("half") ^ flip) * 4 + ((lax.axis_index("mp") + step) & 3)


def columns(place, width):
    return pl.ds(pl.multiple_of(place * width, width if width < 128 else 128), width)


SHARE_MOVES = [(0, 0), (0, 1), (0, 3), (1, 0), (0, 2), (1, 2), (1, 1), (1, 3)]


def split3(value):
    high = value.astype(BF).astype(F32)
    rest = value - high
    mid = rest.astype(BF).astype(F32)
    return high, mid, rest - mid


def message_kernel(queries, keys, values, w_in, w_out_t, frames, *outs):
    kv_out, core_out, y_out, piece_out = outs
    row = jnp.broadcast_to(frames[...].astype(F32), (16, TOK)).astype(BF)
    kv_out[0:TOK, :] = keys[...]
    kv_out[TOK : 2 * TOK, :] = values[...]
    for head in range(HEADS):
        kv_out[2 * TOK : 2 * TOK + 16, head * DH : (head + 1) * DH] = row
    for out in (core_out, y_out):
        out[...] = jnp.zeros_like(out)
        out[0:TOK, 0 : HEADS * DH] = queries[...]
        out[TOK : TOK + 16, 0:TOK] = row
    places = ((piece_out, 0, 0), (core_out, 640, 1), (y_out, 640, 3), (y_out, 896, 2))
    for out, begin, flip in places:
        at = columns(quad_place(flip), 256)
        out[0:64, begin : begin + 256] = w_in[:, at]
        out[64:128, begin : begin + 256] = w_out_t[:, at]


def attend_kernel(*refs):
    q_refs = (refs[0], *refs[2:5])
    kv_refs, far_k, far_v = (refs[1], *refs[5:11]), refs[11], refs[12]
    outs, stat = refs[13:17], refs[17]
    scale = LOG2E / math.sqrt(DH)
    stat[...] = jnp.zeros_like(stat)
    key_frames = jnp.concatenate(
        [r[2 * TOK : 2 * TOK + 16, 0:TOK].astype(F32)[0:1] for r in kv_refs]
        + [far_v[TOK : TOK + 16, 0:TOK].astype(F32)[0:1]],
        axis=1,
    )
    lane = lax.broadcasted_iota(jnp.int32, (TOK, DH), 1)
    query_frames = []
    for ref in q_refs:
        row = ref[TOK : TOK + 16, 0:TOK].astype(F32)[0:1]
        query_frames.append(jnp.transpose(jnp.broadcast_to(row, (DH, TOK)))[:, 0:1])

    def head_step(head, carry):
        at = pl.ds(pl.multiple_of(head * DH, DH), DH)
        key = jnp.concatenate([r[0:TOK, at] for r in kv_refs] + [far_k[:, at]], axis=0)
        val = jnp.concatenate(
            [r[TOK : 2 * TOK, at] for r in kv_refs] + [far_v[0:TOK, at]], axis=0
        )
        for j in range(4):
            query = q_refs[j][0:TOK, at]
            scores = lax.dot_general(
                query, key, (((1,), (1,)), ((), ())), preferred_element_type=F32
            )
            scores = jnp.where(key_frames <= query_frames[j], scores, -1e30)
            top = jnp.maximum(jnp.max(scores, axis=1, keepdims=True), -1e29)
            weights = jnp.exp2((scores - top) * scale)
            total = jnp.sum(weights, axis=1, keepdims=True)
            mixed = lax.dot_general(
                weights.astype(BF), val, (((1,), (0,)), ((), ())), preferred_element_type=F32
            )
            seen = total > 0.0
            safe = jnp.where(seen, total, 1.0)
            outs[j][:, at] = (mixed / safe).astype(BF)
            level = jnp.where(seen, top * scale + jnp.log2(safe), -1e30)
            high, mid, low = split3(level)
            stat[j] += (
                jnp.where(lane == head, high, 0.0)
                + jnp.where(lane == head + 16, mid, 0.0)
                + jnp.where(lane == head + 32, low, 0.0)
            )
        return carry

    lax.fori_loop(0, HEADS, head_step, 0)
    for j in range(4):
        outs[j][:, HEADS * DH :] = stat[j].astype(BF)


def merged(parts):
    stats = [p[:, HEADS * DH :].astype(F32) for p in parts]
    columns = []
    for head in range(HEADS):
        levels = [
            s[:, head : head + 1] + s[:, head + 16 : head + 17] + s[:, head + 32 : head + 33]
            for s in stats
        ]
        top = functools.reduce(jnp.maximum, levels)
        factors = [jnp.exp2(level - top) for level in levels]
        total = sum(factors[1:], factors[0])
        at = slice(head * DH, (head + 1) * DH)
        mixed = sum(f * p[:, at].astype(F32) for f, p in zip(factors, parts))
        columns.append((mixed / total).astype(BF))
    return jnp.concatenate(columns, axis=1)


def project_kernel(weight, *refs):
    parts, outs, held, sems = refs[:4], refs[4:12], refs[12], refs[13]
    copies = []
    for k in range(8):
        at = columns(share_place(*SHARE_MOVES[k]), 640)
        copies.append(pltpu.make_async_copy(weight.at[:, at], held.at[k], sems.at[k]))
        copies[-1].start()
    attended = merged(parts)
    for k, out in enumerate(outs):
        copies[k].wait()
        out[...] = jnp.dot(attended, held[k], preferred_element_type=F32).astype(BF)


def project(weight, *parts):
    vmem = pl.BlockSpec(memory_space=pltpu.VMEM)
    return pl.pallas_call(
        project_kernel,
        in_specs=[pl.BlockSpec(memory_space=pltpu.HBM), *[vmem] * 4],
        out_specs=[vmem] * 8,
        out_shape=[jax.ShapeDtypeStruct((TOK, 640), BF)] * 8,
        scratch_shapes=[pltpu.VMEM((8, 640, 640), BF), pltpu.SemaphoreType.DMA((8,))],
        compiler_params=pltpu.CompilerParams(vmem_limit_bytes=50 * MIB),
        cost_estimate=pl.CostEstimate(flops=840000000, bytes_accessed=9000000, transcendentals=0),
    )(weight, *parts)


def feature_kernel(proj, s_local, s_core, s_y, *refs):
    parts, base, outs = refs[:8], refs[8], refs[9:17]
    feature = base[...]
    for part in parts:
        feature = feature + part[...].astype(F32)
    square = jnp.sum(feature * feature, axis=1, keepdims=True)
    turned = jnp.transpose(jnp.broadcast_to(square, (TOK, TOK)))
    high, mid, low = split3(turned[0:16])
    index = lax.broadcasted_iota(jnp.int32, (16, TOK), 0)
    rows = jnp.where(index == 0, high, jnp.where(index == 1, mid, low))
    rows = jnp.concatenate([rows, rows], axis=1).astype(BF)
    narrow = feature.astype(BF)
    for k, out in enumerate(outs):
        at = columns(share_place(*SHARE_MOVES[k]), 256)
        out[0:TOK, :] = jnp.dot(narrow, proj[:, at], preferred_element_type=F32).astype(BF)
        near = s_local[0:TOK, at].astype(F32) + s_core[0:TOK, at].astype(F32)
        out[TOK : 2 * TOK, :] = (near + s_y[:, at].astype(F32)).astype(BF)
        out[2 * TOK : 2 * TOK + 16, :] = rows


def away_kernel(local, got, out):
    out[...] = (local[TOK:, :].astype(F32) + got[TOK:, :].astype(F32)).astype(BF)


def error_kernel(inputs, *refs):
    parts, out = refs[:8], refs[8]
    student = inputs[:, columns(share_place(0, 0), 256)].astype(F32)
    target, rows = 0.0, 0.0
    for part in parts:
        target = target + part[0:TOK, :].astype(F32)
        student = student + part[TOK : 2 * TOK, :].astype(F32)
        rows = rows + part[2 * TOK : 2 * TOK + 16, :].astype(F32)
    square = rows[0:1, 0:TOK] + rows[1:2, 0:TOK] + rows[2:3, 0:TOK]
    column = jnp.transpose(jnp.broadcast_to(square, (TOK, TOK)))[:, 0:1]
    inverse = lax.rsqrt(column * (1.0 / 5120.0) + 1e-6)
    out[...] = ((student - target * inverse) * (1.0 / 64.0)).astype(BF)


def merge_kernel(own, from_core, from_y, from_both, out):
    blocks = ((own, 0), (from_core, 640), (from_y, 896), (from_both, 640))
    for j, (piece, at) in enumerate(blocks):
        begin = pl.multiple_of(quad_place(j) * 64, 64)
        out[pl.ds(begin, 64), :] = piece[0:64, at : at + 256]
        out[pl.ds(begin + 256, 64), :] = piece[64:128, at : at + 256]


def student_kernel(x0, x1, x2, x3, weight, *rest):
    slope, hidden_t, local, to_core = rest[-4:]
    pre = jnp.zeros((4 * TOK, 256), F32)
    for z in range(8):
        at = slice(z * 256, (z + 1) * 256)
        rows = jnp.concatenate([x0[:, at], x1[:, at], x2[:, at], x3[:, at]], axis=0)
        pre = pre + jnp.dot(rows, weight[z, 0:256, :], preferred_element_type=F32)
    activated, slope[...] = gelu_parts(pre)
    hidden_t[...] = jnp.transpose(activated).astype(BF)
    hidden = activated.astype(BF)
    for z in range(8):
        at = slice(z * 256, (z + 1) * 256)
        spread = lax.dot_general(
            hidden,
            weight[z, 256:512, :],
            (((1,), (1,)), ((), ())),
            preferred_element_type=F32,
        ).astype(BF)
        for a in range(2):
            local[a * TOK : (a + 1) * TOK, at] = spread[2 * a * TOK : (2 * a + 1) * TOK]
            to_core[a * TOK : (a + 1) * TOK, at] = spread[(2 * a + 1) * TOK : (2 * a + 2) * TOK]


def grad_kernel(*refs):
    weight, slope, hidden_t = refs[0:3]
    x_refs = refs[3:7]
    mine = refs[7:11]
    theirs = refs[11:15]
    in_outs, out_outs = refs[15:23], refs[23:31]
    rows = refs[31]
    z = lax.axis_index("z")
    for half, blocks in enumerate((mine, theirs)):
        for k, block in enumerate(blocks):
            for flip in range(2):
                cols = columns(share_place(flip, k), 256)
                for a in range(2):
                    source = (a * 2 + flip) * TOK
                    at = (a * 2 + half) * TOK
                    rows[at : at + TOK, cols] = block[source : source + TOK, :]
    back = jnp.zeros((4 * TOK, 256), F32)
    for y in range(8):
        back = back + jnp.dot(
            rows[:, y * 256 : (y + 1) * 256], weight[y, 256:512, :], preferred_element_type=F32
        )
    grad_pre = jnp.transpose(back * slope[...]).astype(BF)
    for k in range(8):
        at = columns((z + Z_MOVES[k]) & 7, 256)
        inputs = jnp.concatenate([r[:, at] for r in x_refs], axis=0)
        in_outs[k][...] = jnp.dot(grad_pre, inputs, preferred_element_type=F32).astype(BF)
        out_outs[k][...] = jnp.dot(
            hidden_t[...], rows[:, at], preferred_element_type=F32
        ).astype(BF)


def turn_kernel(a0, a1, a2, b0, b1, b2, o0, o1, o2, o3, block):
    for half, (one, two, three) in enumerate(((a0, a1, a2), (b0, b1, b2))):
        total = one[...].astype(F32) + two[...].astype(F32) + three[...].astype(F32)
        block[:, half * 256 : (half + 1) * 256] = jnp.transpose(total)
    for j, out in enumerate((o0, o1, o2, o3)):
        at = columns(quad_place(j), 64)
        out[...] = block[at, :].astype(BF)


def final_kernel(p0, p1, p2, p3, grad_in, grad_out_t):
    for j, part in enumerate((p0, p1, p2, p3)):
        at = columns(quad_place(j), 256)
        piece = part[...].astype(F32)
        grad_in[:, at] = piece[:, 0:256]
        grad_out_t[:, at] = piece[:, 256:512]


Z_MOVES = [4, 3, -3, 2, -2, 1, -1, 0]


def gelu_parts(value):
    k = math.sqrt(2.0 / math.pi)
    square = value * value
    bend = jnp.tanh(k * (value + 0.044715 * value * square))
    out = 0.5 * value * (1.0 + bend)
    slope = 0.5 * (1.0 + bend) + 0.5 * value * (1.0 - bend * bend) * k * (
        1.0 + 3.0 * 0.044715 * square
    )
    return out, slope


def per_device(
    queries,
    keys,
    values,
    token_frames,
    frame_actions,
    teacher_resid,
    out_weight,
    action_table,
    projection,
    student_input,
    w_in,
    w_out,
):
    own_kv, to_core, to_y, own_piece = call(
        message_kernel,
        [
            ((2 * TOK + 16, 640), BF),
            ((TOK + 16, 896), BF),
            ((TOK + 16, 1152), BF),
            ((TOK, 256), BF),
        ],
        fetch=5,
        vmem=60,
    )(queries, keys, values, w_in, w_out.T, token_frames.reshape(1, TOK))
    up1, down1 = z_shift(own_kv, 1), z_shift(own_kv, -1)
    from_y = quad_swap(to_y, 2)
    from_core = quad_swap(to_core, 1)
    from_y, from_core, up1, down1 = lax.optimization_barrier((from_y, from_core, up1, down1))
    up2, down2 = z_shift(up1, 1), z_shift(down1, -1)
    from_both = quad_swap(from_y, 1)
    from_both, up2, down2 = lax.optimization_barrier((from_both, up2, down2))
    (w_block,) = call(merge_kernel, [((512, 256), BF)], size=500000)(
        own_piece, from_core, from_y, from_both
    )
    w_all = lax.all_gather(w_block, "z", axis=0, tiled=False)
    up3, down3 = z_shift(up2, 1), z_shift(down2, -1)
    x_own = lax.optimization_barrier((student_input, up2))[0]
    x_y = quad_swap(x_own, 2)
    x_c = quad_swap(x_own, 1)
    far_k, far_v = z_shift(up3[:TOK], 1), z_shift(down3[TOK:], -1)
    far_k, far_v, x_y, x_c = lax.optimization_barrier((far_k, far_v, x_y, x_c))

    frame_match = token_frames[:, None] == jnp.arange(24, dtype=jnp.int32)[None, :]
    token_action = jnp.sum(jnp.where(frame_match, frame_actions[None, :], 0), axis=1)
    action_hot = (token_action[:, None] == jnp.arange(64, dtype=jnp.int32)[None, :]).astype(BF)
    base = teacher_resid.astype(F32) + jnp.dot(
        action_hot, action_table, preferred_element_type=F32
    )

    partial = call(
        attend_kernel,
        [((TOK, 768), BF)] * 4,
        [pltpu.VMEM((4, TOK, TOK), F32)],
        fetch=2,
        flops=1400000000,
        size=6000000,
    )(
        to_core, own_kv, from_core, from_y, from_both,
        up1, down1, up2, down2, up3, down3, far_k, far_v,
    )
    parts = [partial[0]] + [quad_swap(partial[j], j) for j in (1, 2, 3)]
    x_y, parts[0] = lax.optimization_barrier((x_y, parts[0]))
    x_parts = (student_input, x_c, x_y, quad_swap(x_y, 1))
    slope, hidden_t, local, local_core = call(
        student_kernel,
        [((512, 256), F32), ((256, 512), BF), ((256, 2048), BF), ((256, 2048), BF)],
        fetch=5,
        later=2,
    )(*x_parts, w_all, parts[2], parts[3])
    got_core = quad_swap(local_core, 1)
    (away,) = call(away_kernel, [((TOK, 2048), BF)])(local, got_core)
    got_y = quad_swap(away, 2)
    chunks = project(out_weight, *parts)
    sums = [chunks[0]] + [
        share_shift(c, flip, step) for c, (flip, step) in zip(chunks[1:], SHARE_MOVES[1:])
    ]
    chunks = call(
        feature_kernel,
        [((2 * TOK + 16, 256), BF)] * 8,
        fetch=4,
        vmem=44,
        flops=340000000,
        size=5000000,
    )(projection, local, got_core, got_y, *sums, base)
    sums = [chunks[0]] + [
        share_shift(c, flip, step) for c, (flip, step) in zip(chunks[1:], SHARE_MOVES[1:])
    ]
    (grad_share,) = call(error_kernel, [((TOK, 256), BF)], fetch=1)(
        student_input, *sums
    )

    def y_move(value, flip_high, flip_low):
        pairs = [
            (h * 2 + y, (h ^ flip_low) * 2 + (y ^ flip_high)) for h in range(2) for y in range(2)
        ]
        return lax.ppermute(value, ("half", "yh"), pairs)

    along_y = jnp.concatenate(
        [grad_share, y_move(grad_share, 0, 1), y_move(grad_share, 1, 0), y_move(grad_share, 1, 1)],
        axis=0,
    )
    mine = [along_y] + [
        lax.ppermute(along_y, "mp", [(i, (i - k) % 4) for i in range(4)]) for k in (1, 2, 3)
    ]
    theirs = [quad_swap(m, 1) for m in mine]
    grads = call(
        grad_kernel,
        [((256, 256), BF)] * 16,
        [pltpu.VMEM((512, 2048), BF)],
        fetch=7,
        vmem=44,
        flops=1700000000,
        size=10000000,
    )(w_all, slope, hidden_t, *x_parts, *mine, *theirs)
    grad_a, grad_b = dict(zip(Z_MOVES, grads[:8])), dict(zip(Z_MOVES, grads[8:]))

    def added(one, two):
        return (one.astype(F32) + two.astype(F32)).astype(BF)

    up_a, down_b = z_shift(grad_a[4], 1), z_shift(grad_b[4], -1)
    up_b, down_a = z_shift(grad_b[3], 1), z_shift(grad_a[-3], -1)
    up_a, down_b = z_shift(added(up_a, grad_a[3]), 1), z_shift(added(down_b, grad_b[-3]), -1)
    for k in (2, 1):
        up_b = z_shift(added(up_b, grad_b[k]), 1)
        down_a = z_shift(added(down_a, grad_a[-k]), -1)
        up_a = z_shift(added(up_a, grad_a[k]), 1)
        down_b = z_shift(added(down_b, grad_b[-k]), -1)
    blocks = call(
        turn_kernel,
        [((64, 512), BF)] * 4,
        [pltpu.VMEM((256, 512), F32)],
        flops=1000000,
        size=1000000,
    )(grad_a[0], up_a, down_a, grad_b[0], up_b, down_b)
    blocks = [blocks[0]] + [quad_swap(blocks[j], j) for j in (1, 2, 3)]
    grad_in, grad_out_t = call(
        final_kernel, [((64, 1024), F32)] * 2, flops=1000000, size=1000000
    )(*blocks)
    return grad_in, grad_out_t.T


def solution(mesh):
    shape = mesh.devices.shape
    fine = Mesh(
        mesh.devices.reshape(shape[0], 8, 2, 2, shape[2]), ("half", "z", "yh", "core", "mp")
    )
    ctx = ("z", "yh", "core")
    share = ("half", "mp")
    return jax.shard_map(
        per_device,
        mesh=fine,
        in_specs=(
            P(ctx, share),
            P(ctx, share),
            P(ctx, share),
            P(ctx),
            P(),
            P(ctx, share),
            P(share, None),
            P(None, share),
            P(share, None),
            P(ctx, None),
            P(ctx, share),
            P(share, ctx),
        ),
        out_specs=(P(ctx, share), P(share, ctx)),
        check_vma=False,
    )
```
